32 devices in a mesh: comp: 4 (over x, core), tile: 8 (over z, y).
Axes of the slice: x: 2, y: 2, z: 4, core: 2. Of those that a mesh axis runs over, the one named last changes fastest.
Arguments:
- forcing: float32 [4, 8, 16, 256, 128], P('comp', None, None, 'tile'), may hold values from -6 to 6
- kappa: float32 [4, 256, 128], P('comp', 'tile'), may hold values from 0.02 to 0.24
- col_blocks: int32 [4, 128, 4], P('comp', 'tile'), may hold values from 0 to 127, as said below
- remap_weights: bfloat16 [4, 128, 4, 256, 256], P('comp', 'tile'), may hold values from -0.1875 to 0.1875
Outputs:
- section_out: bfloat16 [4, 8, 16, 256, 128], P('comp', None, None, 'tile')
The draws below stay inside these ranges and needn't reach their ends.
Inputs may be any that keep to these rules, and one draw needn't show every extreme that they name: `col_blocks`: the first column block of row block j is j itself; every column block lies within 8 blocks of its row block, cyclically over the 128 blocks; in every row block one lies exactly 8 blocks away.
All inputs are finite; a program needn't handle non-finite values.
Results may differ from the reference program's by a relative error of at most 0.0055.
Values may be sent and summed in bfloat16 or wider, within the bound.
No kernel may reach another device: no remote copies, remote signals or barrier semaphores. Data moves between devices by JAX's collectives and lax.ppermute only.
A program may use at most 64 MiB of HBM per device.

```python
import math
import jax
import jax.numpy as jnp
from jax import lax

F = 16
TX = 128
MB = 8
NB = 4
BLK = 256
HALF = 8
NBLK = 128
NY = 256
SECTIONS = 4


def draw_col_blocks(key, part):
    base = jax.random.fold_in(key, 11)
    key_sign, key_rest = jax.random.split(base, 2)
    row_ids = jnp.arange(NBLK, dtype=jnp.int32)
    far_sign = jax.random.randint(key_sign, (SECTIONS, NBLK), 0, 2).astype(jnp.int32) * 2 - 1
    far_offset = far_sign * HALF
    rest_offset = jax.random.randint(key_rest, (SECTIONS, NBLK, NB - 2), -HALF, HALF + 1).astype(jnp.int32)
    offsets = jnp.concatenate([jnp.zeros((SECTIONS, NBLK, 1), jnp.int32), far_offset[:, :, None], rest_offset], axis=2)
    return jnp.mod(row_ids[None, :, None] + offsets, NBLK).astype(jnp.int32)


def shard_levels(key, dims, pieces, low, high):
    gain = 1.0
    for dim, shards_of in pieces:
        steps = jax.random.uniform(jax.random.fold_in(jax.random.fold_in(key, 6), dim), (shards_of,), jnp.float32, low / len(pieces), high / len(pieces))
        gain = gain * jnp.repeat(jnp.exp(steps), dims[dim] // shards_of).reshape((-1,) + (1,) * (len(dims) - 1 - dim))
    return gain


def centred(stream_key, extent, width, most, pieces=(), kind=jnp.bfloat16):
    array = width * jax.random.normal(stream_key, extent, jnp.float32)
    if pieces:
        array = array * shard_levels(stream_key, extent, pieces, -0.22, 0.18)
    return jnp.clip(array, -most, most).astype(kind)


def setup_inputs(seed: int = 0) -> dict:
    streams_of = jax.random.split(jax.random.key(seed), 5)
    forcing = centred(streams_of[0], (SECTIONS, MB, F, NY, TX), 1.0, 6.0, ((0, 4), (3, 8)), jnp.float32)
    kappa = jnp.clip(jnp.exp(math.log(0.24) - 2.4849066 * jax.random.uniform(streams_of[1], (SECTIONS, NY, TX), jnp.float32) ** shard_levels(streams_of[1], (SECTIONS, NY, TX), ((0, 4), (1, 8)), -0.2, 0.2)), 0.02, 0.24)
    col_blocks = draw_col_blocks(jax.random.fold_in(streams_of[4], 71), 0)
    remap_weights = centred(streams_of[3], (SECTIONS, NBLK, NB, BLK, BLK), (NB * BLK) ** -0.5, 0.1875, ((0, 4), (1, 8)))
    return dict(forcing=forcing, kappa=kappa, col_blocks=col_blocks, remap_weights=remap_weights)


def smooth_step(values, coefficient):
    padded = jnp.pad(values, [(0, 0)] * (values.ndim - 2) + [(1, 1), (0, 0)])
    beside_all = padded[..., :-2, :] + padded[..., 2:, :] + jnp.roll(values, 1, -1) + jnp.roll(values, -1, -1)
    return values + coefficient * (beside_all - 4.0 * values)


def remap_single(sources, columns, weights):
    blocks = sources.reshape(sources.shape[0], NBLK, BLK)
    picked = blocks[:, columns].astype(jnp.float32)
    result = jnp.einsum("fjkc,jkrc->fjr", picked, weights)
    return result.reshape(sources.shape).astype(jnp.bfloat16)


def reference(forcing, kappa, col_blocks, remap_weights):
    incoming = jnp.zeros(forcing.shape[1:], jnp.float32)
    results = []
    for section_num in range(SECTIONS):
        coefficient = kappa[section_num]
        values = forcing[section_num] + incoming
        values = smooth_step(values, coefficient)
        values = smooth_step(values, coefficient)
        sources = values.astype(jnp.bfloat16)
        weights = remap_weights[section_num].astype(jnp.float32)
        columns = col_blocks[section_num]

        def inner(single):
            return remap_single(single, columns, weights)

        mapped = lax.map(inner, sources)
        results.append(mapped)
        incoming = mapped.astype(jnp.float32)
    return jnp.stack(results)
```

```python
import functools

import jax
import jax.numpy as jnp
from jax import lax
from jax.experimental import pallas as pl
from jax.experimental.pallas import tpu as pltpu
from jax.sharding import PartitionSpec as P

AXES = ("comp", "tile")
CHUNKS = 1
EDGE = 2


def diffuse(center, north, south, coefficient):
    cells = center.shape[1]
    beside = pltpu.roll(center, 1, 1) + pltpu.roll(center, cells - 1, 1)
    return center + coefficient * ((north + south) + (beside - 4.0 * center))


def section_kernel(
    chunk, has_incoming, has_next, group,
    flags, offsets, kappa, forcing, *refs,
):
    refs = list(refs)
    incoming = refs.pop(0) if has_incoming else None
    upper, lower = refs.pop(0), refs.pop(0)
    following = refs.pop(0) if has_next else None
    weights, _ = refs.pop(0), refs.pop(0)
    kept = refs.pop(0)
    if has_next:
        own_out, up_out, down_out = refs.pop(0), refs.pop(0), refs.pop(0)
    (f_v, in_v, up_v, down_v, next_v, w_v, smooth, own_v, up_s, down_s, sems, w_sems) = refs
    rows, fields, cells = f_v.shape
    halo = up_v.shape[0]
    count, per_row = w_v.shape[:2]
    block = w_v.shape[-1]
    extent = rows + 2 * halo
    lo, hi = halo, halo + rows

    @pl.when(flags[0] == 1)
    def _():
        mine = pl.ds(chunk * fields, fields)
        loads = [
            pltpu.make_async_copy(upper, up_v, sems.at[0]),
            pltpu.make_async_copy(forcing.at[:, mine], f_v, sems.at[1]),
            pltpu.make_async_copy(lower, down_v, sems.at[2]),
        ]
        if has_incoming:
            loads.append(pltpu.make_async_copy(incoming, in_v, sems.at[3]))
        if has_next:
            late = pltpu.make_async_copy(following.at[:, mine], next_v, sems.at[4])
        for copy in loads:
            copy.start()
        w_loads = [pltpu.make_async_copy(weights.at[j], w_v.at[j], w_sems.at[j]) for j in range(count)]
        for copy in w_loads:
            copy.start()
        if has_next:
            late.start()
        for copy in loads:
            copy.wait()

        top = jnp.where(flags[1] == 1, 0.0, 1.0)
        bottom = jnp.where(flags[2] == 1, 0.0, 1.0)

        def per_group(g, _):
            part = pl.ds(pl.multiple_of(g * group, group), group)

            def entry(i, where):
                if where == 0:
                    return up_v[i, part, :].astype(jnp.float32)
                if where == 2:
                    return down_v[i - hi, part, :].astype(jnp.float32)
                value = f_v[i - lo, part, :]
                if has_incoming:
                    value = value + in_v[i - lo, part, :].astype(jnp.float32)
                return value

            def masked(i, north, south):
                if isinstance(i, int):
                    if i == lo:
                        north = north * top
                    if i == lo - 1:
                        south = south * top
                    if i == hi:
                        north = north * bottom
                    if i == hi - 1:
                        south = south * bottom
                return north, south

            def first_step(i, e_before, e_here, e_after):
                north, south = masked(i, e_before, e_after)
                return diffuse(e_here, north, south, kappa[pl.ds(i, 1), :])

            def advance(i, where, parity, carry):
                e_before, e_here, d_before, d_here = carry
                e_after = entry(i + 1, where)
                d_after = first_step(i, e_before, e_here, e_after)
                if parity is not None:
                    north, south = masked(i - 1 if isinstance(i, int) else None, d_before, d_after)
                    result = diffuse(d_here, north, south, kappa[pl.ds(i - 1, 1), :])
                    out = i - 3
                    smooth[out // 2, part, parity * cells:(parity + 1) * cells] = result.astype(jnp.bfloat16)
                return e_here, e_after, d_here, d_after

            def span(start, stop, where, carry):
                def pair(p, carry):
                    carry = advance(start + 2 * p, where, 0, carry)
                    return advance(start + 2 * p + 1, where, 1, carry)

                return lax.fori_loop(0, (stop - start) // 2, pair, carry)

            def around(edge, where, carry):
                for i in range(edge - 1, edge + 3):
                    carry = advance(i, where, (i - 3) % 2, carry)
                return carry

            carry = (entry(0, 0), entry(1, 0), None, None)
            zero = jnp.zeros_like(carry[0])
            carry = (carry[0], carry[1], zero, zero)
            carry = advance(1, 0, None, carry)
            carry = advance(2, 0, None, carry)
            carry = span(3, lo - 1, 0, carry)
            carry = around(lo, 1, carry)
            carry = span(lo + 3, hi - 1, 1, carry)
            carry = around(hi, 2, carry)
            span(hi + 3, extent - 1, 2, carry)
            return 0

        lax.fori_loop(0, fields // group, per_group, 0)

        if has_next:
            late.wait()
        half = (halo - EDGE) * cells // block
        block_rows = block // cells
        for j in range(count):
            w_loads[j].wait()
            total = None
            for k in range(per_row):
                source = smooth[offsets[j, k] + (j + half)]
                term = lax.dot_general(
                    source, w_v[j, k], (((1,), (1,)), ((), ())), preferred_element_type=jnp.float32
                )
                total = term if total is None else total + term
            for r in range(block_rows):
                row = j * block_rows + r
                value = total[:, r * cells:(r + 1) * cells].astype(jnp.bfloat16)
                own_v[row] = value
                if has_next:
                    if row < halo or row >= rows - halo:
                        entry_next = (value.astype(jnp.float32) + next_v[row].astype(jnp.float32)).astype(jnp.bfloat16)
                    if row < halo:
                        up_s[row] = entry_next
                    if row >= rows - halo:
                        down_s[row - (rows - halo)] = entry_next
        stores = [pltpu.make_async_copy(own_v, kept.at[:, mine], sems.at[0])]
        if has_next:
            stores.append(pltpu.make_async_copy(own_v, own_out, sems.at[1]))
            stores.append(pltpu.make_async_copy(up_s, up_out, sems.at[2]))
            stores.append(pltpu.make_async_copy(down_s, down_out, sems.at[3]))
        for copy in stores:
            copy.start()
        for copy in stores:
            copy.wait()


def section(chunk, flags, offsets, kappa, forcing, incoming, upper, lower, following, weights, kept):
    rows, total, cells = forcing.shape
    halo, fields, _ = upper.shape
    count, per_row, block, _ = weights.shape
    has_incoming, has_next = incoming is not None, following is not None
    any_spec = pl.BlockSpec(memory_space=pl.ANY)
    smem = pl.BlockSpec(memory_space=pltpu.SMEM)
    operands = [flags, offsets, kappa, forcing]
    specs = [smem, smem, pl.BlockSpec(memory_space=pltpu.VMEM), any_spec]
    for value in (incoming, upper, lower, following, weights, kept):
        if value is not None:
            operands.append(value)
            specs.append(any_spec)
    outs = [jax.ShapeDtypeStruct(kept.shape, jnp.bfloat16)]
    if has_next:
        outs.append(jax.ShapeDtypeStruct((rows, fields, cells), jnp.bfloat16))
        outs.append(jax.ShapeDtypeStruct((halo, fields, cells), jnp.bfloat16))
        outs.append(jax.ShapeDtypeStruct((halo, fields, cells), jnp.bfloat16))
    blocks = (rows + 2 * (halo - EDGE)) * cells // block
    group = min(fields, 32)
    return pl.pallas_call(
        functools.partial(section_kernel, chunk, has_incoming, has_next, group),
        in_specs=specs,
        out_shape=outs,
        out_specs=[any_spec] * len(outs),
        input_output_aliases={len(operands) - 1: 0},
        scratch_shapes=[
            pltpu.VMEM((rows, fields, cells), jnp.float32),
            pltpu.VMEM((rows, fields, cells), jnp.bfloat16),
            pltpu.VMEM((halo, fields, cells), jnp.bfloat16),
            pltpu.VMEM((halo, fields, cells), jnp.bfloat16),
            pltpu.VMEM((rows, fields, cells), jnp.bfloat16),
            pltpu.VMEM(weights.shape, jnp.bfloat16),
            pltpu.VMEM((blocks, fields, block), jnp.bfloat16),
            pltpu.VMEM((rows, fields, cells), jnp.bfloat16),
            pltpu.VMEM((halo, fields, cells), jnp.bfloat16),
            pltpu.VMEM((halo, fields, cells), jnp.bfloat16),
            pltpu.SemaphoreType.DMA((5,)),
            pltpu.SemaphoreType.DMA((count,)),
        ],
        compiler_params=pltpu.CompilerParams(vmem_limit_bytes=40 << 20),
        cost_estimate=pl.CostEstimate(
            flops=2 * count * per_row * block * block * fields,
            bytes_accessed=weights.size * 2 + 8 * rows * fields * cells,
            transcendentals=0,
        ),
    )(*operands)


def local(forcing, kappa, col_blocks, remap_weights):
    n_tile = lax.axis_size("tile")
    n_section = lax.axis_size("comp")
    tile_pos = lax.axis_index("tile")
    section_pos = lax.axis_index("comp")
    weights = remap_weights[0]
    count, block = weights.shape[0], weights.shape[-1]
    rows, cells = forcing.shape[-2:]
    half = count // 2
    halo = half * block // cells + EDGE
    total_blocks = count * n_tile
    global_block = tile_pos * count + jnp.arange(count, dtype=jnp.int32)
    offsets = jnp.mod(col_blocks[0] - global_block[:, None] + half, total_blocks) - half
    fields = forcing.reshape(-1, rows, cells)
    n_field = fields.shape[0] // CHUNKS

    def place(s, t):
        return s * n_tile + t % n_tile

    def send(value, source, target, shift):
        return lax.ppermute(value, AXES, [(place(source, t), place(target, t + shift)) for t in range(n_tile)])

    by_row = jnp.transpose(fields, (1, 0, 2))
    narrow = by_row.astype(jnp.bfloat16)
    arrivals = []
    for c in range(CHUNKS):
        part = narrow[:, c * n_field:(c + 1) * n_field]
        arrivals.append((None, send(part[rows - halo:], 0, 0, 1), send(part[:halo], 0, 0, -1)))
    around = [(i, (i + 1) % n_tile) for i in range(n_tile)]
    back = [((i + 1) % n_tile, i) for i in range(n_tile)]
    k_here = kappa[0]
    k_all = jnp.concatenate([
        lax.ppermute(k_here[rows - halo:], "tile", around),
        k_here,
        lax.ppermute(k_here[:halo], "tile", back),
    ])
    following = lax.ppermute(
        narrow, AXES, [(place(s, t), place(s - 1, t)) for s in range(1, n_section) for t in range(n_tile)]
    )
    kept = jnp.zeros(narrow.shape, jnp.bfloat16)
    for s in range(n_section):
        flags = jnp.stack([section_pos == s, tile_pos == 0, tile_pos == n_tile - 1]).astype(jnp.int32)
        last = s + 1 == n_section
        leaving = []
        for c in range(CHUNKS):
            incoming, upper, lower = arrivals[c]
            result = section(
                c, flags, offsets, k_all, by_row, incoming, upper, lower,
                None if last else following, weights, kept,
            )
            kept = result[0]
            if not last:
                own, up, down = result[1:]
                leaving.append((send(own, s, s + 1, 0), send(down, s, s + 1, 1), send(up, s, s + 1, -1)))
        arrivals = leaving
    return jnp.transpose(kept, (1, 0, 2)).reshape(forcing.shape)


def solution(mesh):
    placed = (
        P("comp", None, None, "tile", None),
        P("comp", "tile", None),
        P("comp", "tile", None),
        P("comp", "tile", None, None, None),
    )
    return jax.shard_map(
        local,
        mesh=mesh,
        in_specs=placed,
        out_specs=P("comp", None, None, "tile", None),
        check_vma=False,
    )
```

```python
import functools

import jax
import jax.numpy as jnp
from jax import lax
from jax.experimental import pallas as pl
from jax.experimental.pallas import tpu as pltpu
from jax.sharding import PartitionSpec as P

AXES = ("comp", "tile")
CHUNKS = 2
EDGE = 2
LIMIT = 24 << 20
HBM = pl.BlockSpec(memory_space=pltpu.HBM)
VMEM = pl.BlockSpec(memory_space=pltpu.VMEM)
SMEM = pl.BlockSpec(memory_space=pltpu.SMEM)


def start_all(copies):
    for copy in copies:
        copy.start()


def wait_all(copies):
    for copy in copies:
        copy.wait()


def prepare_kernel(forcing, by_row, narrow, *refs):
    edges, (f_v, n_v, in_sems, out_sems, n_sems) = refs[:-5], refs[-5:]
    rows = f_v.shape[0]
    halo, fields, _ = edges[0].shape
    loads = [pltpu.make_async_copy(forcing.at[:, y], f_v.at[y], in_sems.at[y]) for y in range(rows)]
    start_all(loads)
    stores = []
    for y in range(rows):
        loads[y].wait()
        stores.append(pltpu.make_async_copy(f_v.at[y], by_row.at[y], out_sems.at[y]))
        stores[-1].start()
        n_v[y] = f_v[y].astype(jnp.bfloat16)
    late = [pltpu.make_async_copy(n_v, narrow, n_sems.at[0])]
    for c in range(len(edges) // 2):
        mine = pl.ds(c * fields, fields)
        late.append(pltpu.make_async_copy(n_v.at[pl.ds(0, halo), mine], edges[2 * c], n_sems.at[2 * c + 1]))
        late.append(pltpu.make_async_copy(n_v.at[pl.ds(rows - halo, halo), mine], edges[2 * c + 1], n_sems.at[2 * c + 2]))
    start_all(late)
    wait_all(stores + late)


def prepare(fields, halo):
    total, rows, cells = fields.shape
    n = total // CHUNKS
    edge = jax.ShapeDtypeStruct((halo, n, cells), jnp.bfloat16)
    return pl.pallas_call(
        prepare_kernel,
        in_specs=[HBM],
        out_shape=[
            jax.ShapeDtypeStruct((rows, total, cells), jnp.float32),
            jax.ShapeDtypeStruct((rows, total, cells), jnp.bfloat16),
        ] + [edge] * (2 * CHUNKS),
        out_specs=[HBM] * (2 + 2 * CHUNKS),
        scratch_shapes=[
            pltpu.VMEM((rows, total, cells), jnp.float32),
            pltpu.VMEM((rows, total, cells), jnp.bfloat16),
            pltpu.SemaphoreType.DMA((rows,)),
            pltpu.SemaphoreType.DMA((rows,)),
            pltpu.SemaphoreType.DMA((2 * CHUNKS + 1,)),
        ],
        compiler_params=pltpu.CompilerParams(vmem_limit_bytes=LIMIT),
        cost_estimate=pl.CostEstimate(flops=0, bytes_accessed=fields.size * 12, transcendentals=0),
    )(fields)


def beside_matrix(cells):
    source = lax.broadcasted_iota(jnp.int32, (2 * cells, 2 * cells), 0)
    target = lax.broadcasted_iota(jnp.int32, (2 * cells, 2 * cells), 1)
    apart = (source - target + 2 * cells) % cells
    same = (source < cells) == (target < cells)
    return jnp.where(same & ((apart == 1) | (apart == cells - 1)), 1.0, 0.0).astype(jnp.bfloat16)


def section_kernel(chunk, has_incoming, has_next, flags, offsets, kappa, forcing, *refs):
    refs = list(refs)
    incoming = refs.pop(0) if has_incoming else None
    upper, lower = refs.pop(0), refs.pop(0)
    following = refs.pop(0) if has_next else None
    weights, own_out = refs.pop(0), refs.pop(0)
    if has_next:
        up_out, down_out = refs.pop(0), refs.pop(0)
    once, smooth = refs
    halo, fields, cells = upper.shape
    rows = forcing.shape[0]
    count, per_row = weights.shape[:2]
    block = weights.shape[-1]
    extent = rows + 2 * halo
    lo, hi = halo, halo + rows

    @pl.when(flags[0] == 1)
    def _():
        mine = slice(chunk * fields, (chunk + 1) * fields)
        beside = beside_matrix(cells)
        top = jnp.where(flags[1] == 1, 0.0, 1.0)
        bottom = jnp.where(flags[2] == 1, 0.0, 1.0)

        def entry(i):
            if i < lo:
                return upper[i].astype(jnp.float32)
            if i >= hi:
                return lower[i - hi].astype(jnp.float32)
            value = forcing[i - lo, mine]
            if has_incoming:
                value = value + incoming[i - lo].astype(jnp.float32)
            return value

        def step(i, here, north, south, east_west):
            if i == lo:
                north = north * top
            if i == lo - 1:
                south = south * top
            if i == hi:
                north = north * bottom
            if i == hi - 1:
                south = south * bottom
            return here + kappa[i:i + 1, :] * ((north + south) + (east_west - 4.0 * here))

        def pair_beside(first, second):
            joined = jnp.concatenate([first.astype(jnp.bfloat16), second.astype(jnp.bfloat16)], axis=1)
            total = jnp.dot(joined, beside, preferred_element_type=jnp.float32)
            return total[:, :cells], total[:, cells:]

        there, after = None, entry(0)
        for i in range(0, extent, 2):
            before, here, there = there, after, entry(i + 1)
            after = entry(i + 2) if i + 2 < extent else None
            ew_here, ew_there = pair_beside(here, there)
            if i > 0:
                once[i] = step(i, here, before, there, ew_here)
            if i + 2 < extent:
                once[i + 1] = step(i + 1, there, here, after, ew_there)
        for i in range(2, extent - 2, 2):
            here, there = once[i], once[i + 1]
            ew_here, ew_there = pair_beside(here, there)
            out = i // 2 - 1
            smooth[out, :, :cells] = step(i, here, once[i - 1], there, ew_here).astype(jnp.bfloat16)
            smooth[out, :, cells:] = step(i + 1, there, here, once[i + 2], ew_there).astype(jnp.bfloat16)

        half = (halo - EDGE) * cells // block
        block_rows = block // cells
        for j in range(count):
            total = None
            for k in range(per_row):
                source = smooth[offsets[j, k] + (j + half)]
                term = lax.dot_general(
                    source, weights[j, k], (((1,), (1,)), ((), ())), preferred_element_type=jnp.float32
                )
                total = term if total is None else total + term
            for r in range(block_rows):
                row = j * block_rows + r
                value = total[:, r * cells:(r + 1) * cells].astype(jnp.bfloat16)
                own_out[row] = value
                if has_next:
                    entry_next = value.astype(jnp.float32) + following[row, mine].astype(jnp.float32)
                    if row < halo:
                        up_out[row] = entry_next.astype(jnp.bfloat16)
                    if row >= rows - halo:
                        down_out[row - (rows - halo)] = entry_next.astype(jnp.bfloat16)


def section(chunk, flags, offsets, kappa, forcing, incoming, upper, lower, following, weights):
    rows, total, cells = forcing.shape
    halo, fields, _ = upper.shape
    count, per_row, block, _ = weights.shape
    has_incoming, has_next = incoming is not None, following is not None
    operands = [flags, offsets]
    for value in (kappa, forcing, incoming, upper, lower, following, weights):
        if value is not None:
            operands.append(value)
    outs = [jax.ShapeDtypeStruct((rows, fields, cells), jnp.bfloat16)]
    if has_next:
        outs.append(jax.ShapeDtypeStruct((halo, fields, cells), jnp.bfloat16))
        outs.append(jax.ShapeDtypeStruct((halo, fields, cells), jnp.bfloat16))
    extent = rows + 2 * halo
    return pl.pallas_call(
        functools.partial(section_kernel, chunk, has_incoming, has_next),
        in_specs=[SMEM] * 2 + [VMEM] * (len(operands) - 2),
        out_shape=outs,
        out_specs=[VMEM] * len(outs),
        scratch_shapes=[
            pltpu.VMEM((extent, fields, cells), jnp.float32),
            pltpu.VMEM(((extent - 2 * EDGE) * cells // block, fields, block), jnp.bfloat16),
        ],
        compiler_params=pltpu.CompilerParams(vmem_limit_bytes=LIMIT),
        cost_estimate=pl.CostEstimate(
            flops=2 * count * per_row * block * block * fields,
            bytes_accessed=weights.size * 2 + 8 * rows * fields * cells,
            transcendentals=0,
        ),
    )(*operands)


def local(forcing, kappa, col_blocks, remap_weights):
    n_tile = lax.axis_size("tile")
    n_section = lax.axis_size("comp")
    tile_pos = lax.axis_index("tile")
    section_pos = lax.axis_index("comp")
    weights = remap_weights[0]
    count, block = weights.shape[0], weights.shape[-1]
    rows, cells = forcing.shape[-2:]
    half = count // 2
    halo = half * block // cells + EDGE
    total_blocks = count * n_tile
    global_block = tile_pos * count + jnp.arange(count, dtype=jnp.int32)
    offsets = jnp.mod(col_blocks[0] - global_block[:, None] + half, total_blocks) - half

    def place(s, t):
        return s * n_tile + t % n_tile

    def send(value, source, target, shift):
        return lax.ppermute(value, AXES, [(place(source, t), place(target, t + shift)) for t in range(n_tile)])

    by_row, narrow, *edges = prepare(forcing.reshape(-1, rows, cells), halo)
    arrivals = []
    for c in range(CHUNKS):
        first, last = edges[2 * c:2 * c + 2]
        arrivals.append((None, send(last, 0, 0, 1), send(first, 0, 0, -1)))
    around = [(i, (i + 1) % n_tile) for i in range(n_tile)]
    back = [((i + 1) % n_tile, i) for i in range(n_tile)]
    k_here = kappa[0]
    k_all = jnp.concatenate([
        lax.ppermute(k_here[rows - halo:], "tile", around),
        k_here,
        lax.ppermute(k_here[:halo], "tile", back),
    ])
    following = lax.ppermute(
        narrow, AXES, [(place(s, t), place(s - 1, t)) for s in range(1, n_section) for t in range(n_tile)]
    )
    results = []
    for s in range(n_section):
        flags = jnp.stack([section_pos == s, tile_pos == 0, tile_pos == n_tile - 1]).astype(jnp.int32)
        last = s + 1 == n_section
        leaving = []
        for c in range(CHUNKS):
            incoming, upper, lower = arrivals[c]
            result = section(
                c, flags, offsets, k_all, by_row, incoming, upper, lower, None if last else following, weights
            )
            own = result[0]
            results.append(own if s == 0 else jnp.where(section_pos == s, own, results[-CHUNKS]))
            if not last:
                up, down = result[1:]
                leaving.append((send(own, s, s + 1, 0), send(down, s, s + 1, 1), send(up, s, s + 1, -1)))
        arrivals = leaving
    kept = jnp.concatenate(results[-CHUNKS:], axis=1)
    return jnp.transpose(kept, (1, 0, 2)).reshape(forcing.shape)


def solution(mesh):
    placed = (
        P("comp", None, None, "tile", None),
        P("comp", "tile", None),
        P("comp", "tile", None),
        P("comp", "tile", None, None, None),
    )
    return jax.shard_map(
        local,
        mesh=mesh,
        in_specs=placed,
        out_specs=P("comp", None, None, "tile", None),
        check_vma=False,
    )
```

```python
import functools

import jax
import jax.numpy as jnp
from jax import lax
from jax.experimental import pallas as pl
from jax.experimental.pallas import tpu as pltpu
from jax.sharding import PartitionSpec as P

AXES = ("comp", "tile")
CHUNKS = 2
EDGE = 2
LIMIT = 24 << 20
FLOPS = 20
HBM = pl.BlockSpec(memory_space=pltpu.HBM)
VMEM = pl.BlockSpec(memory_space=pltpu.VMEM)
ANY = pl.BlockSpec(memory_space=pl.ANY)
SMEM = pl.BlockSpec(memory_space=pltpu.SMEM)


def start_all(copies):
    for copy in copies:
        copy.start()


def wait_all(copies):
    for copy in copies:
        copy.wait()


def turn(forcing, f_v, sems, use):
    rows = f_v.shape[1]
    step = rows // sems.shape[0]
    loads = []
    for i in range(sems.shape[0]):
        part = pl.ds(i * step, step)
        loads.append(pltpu.make_async_copy(forcing.at[:, part], f_v.at[:, part], sems.at[i]))
    start_all(loads)
    for i, load in enumerate(loads):
        load.wait()
        use(i * step, jnp.swapaxes(f_v[:, i * step:(i + 1) * step, :], 0, 1))


def prepare_kernel(forcing, kappa, narrow, *refs):
    edges, (f_v, n_v, k_v, pack_v, pack, sems, out_sems) = refs[:-7], refs[-7:]
    total, rows, cells = f_v.shape
    halo, fields = edges[0].shape[0] - 1, edges[0].shape[1]

    def use(start, part):
        n_v[start:start + part.shape[0]] = part.astype(jnp.bfloat16)

    fetch = pltpu.make_async_copy(kappa, k_v, out_sems.at[0])
    fetch.start()
    turn(forcing, f_v, sems, use)
    fetch.wait()
    stores = []
    for c in range(len(edges) // 2):
        mine = pl.ds(c * fields, fields)
        for e, start in enumerate((0, rows - halo)):
            edge = edges[2 * c + e]
            stores.append((n_v.at[pl.ds(start, halo), mine], edge.at[pl.ds(0, halo)]))
            stores.append((pack.at[e, pl.ds(0, fields)], edge.at[halo]))
    stores.append((n_v, narrow.at[pl.ds(0, rows)]))
    stores.append((pack.at[2], narrow.at[rows]))
    stores = [pltpu.make_async_copy(*pair, out_sems.at[i]) for i, pair in enumerate(stores)]
    start_all(stores[0::2])
    parts = split(k_v[...])
    for e, (start, stop) in enumerate(((0, halo), (rows - halo, rows), (0, rows))):
        pack[e] = joined([part[start:stop] for part in parts], pack_v)
    start_all(stores[1::2])
    wait_all(stores)


def split(value):
    parts = []
    for _ in range(3):
        head = value.astype(jnp.bfloat16).astype(jnp.float32)
        parts.append(head)
        value = value - head
    return parts


def joined(parts, room):
    room[...] = jnp.zeros(room.shape, jnp.float32)
    at = 0
    for part in parts:
        room[at:at + part.shape[0], :] = part
        at += part.shape[0]
    return room[...].astype(jnp.bfloat16)


def prepare(fields, kappa, halo):
    total, rows, cells = fields.shape
    n = total // CHUNKS
    edge = pltpu.HBM((halo + 1, n, cells), jnp.bfloat16)
    return pl.pallas_call(
        prepare_kernel,
        in_specs=[HBM, HBM],
        out_shape=[pltpu.HBM((rows + 1, total, cells), jnp.bfloat16)] + [edge] * (2 * CHUNKS),
        out_specs=[HBM] * (1 + 2 * CHUNKS),
        scratch_shapes=[
            pltpu.VMEM((total, rows, cells), jnp.float32),
            pltpu.VMEM((rows, total, cells), jnp.bfloat16),
            pltpu.VMEM(kappa.shape, kappa.dtype),
            pltpu.VMEM((total, cells), jnp.float32),
            pltpu.VMEM((3, total, cells), jnp.bfloat16),
            pltpu.SemaphoreType.DMA((rows // 8,)),
            pltpu.SemaphoreType.DMA((2 + 4 * CHUNKS,)),
        ],
        compiler_params=pltpu.CompilerParams(vmem_limit_bytes=LIMIT),
        cost_estimate=pl.CostEstimate(flops=0, bytes_accessed=fields.size * 12, transcendentals=0),
    )(*(pltpu.with_memory_space_constraint(value, pltpu.HBM) for value in (fields, kappa)))


def load_kernel(weights, forcing, *refs):
    held, by_row, f_v, sems, sem = refs[-5:]
    copy = pltpu.make_async_copy(weights, held, sem)

    def use(start, part):
        by_row[start:start + part.shape[0]] = part
        if start == 0:
            copy.start()

    turn(forcing, f_v, sems, use)
    copy.wait()


def load(weights, fields, after):
    total, rows, cells = fields.shape
    return pl.pallas_call(
        load_kernel,
        in_specs=[HBM] * 2 + [ANY] * len(after),
        out_shape=[pltpu.VMEM(weights.shape, weights.dtype), pltpu.VMEM((rows, total, cells), fields.dtype)],
        out_specs=[VMEM, VMEM],
        scratch_shapes=[
            pltpu.VMEM((total, rows, cells), jnp.float32),
            pltpu.SemaphoreType.DMA((rows // 8,)),
            pltpu.SemaphoreType.DMA,
        ],
        compiler_params=pltpu.CompilerParams(vmem_limit_bytes=LIMIT),
        cost_estimate=pl.CostEstimate(flops=0, bytes_accessed=weights.size * 4, transcendentals=0),
    )(*(pltpu.with_memory_space_constraint(value, pltpu.HBM) for value in (weights, fields)), *after)


def beside_matrix(cells):
    source = lax.broadcasted_iota(jnp.int32, (2 * cells, 2 * cells), 0)
    target = lax.broadcasted_iota(jnp.int32, (2 * cells, 2 * cells), 1)
    apart = (source - target + 2 * cells) % cells
    same = (source < cells) == (target < cells)
    return jnp.where(same & ((apart == 1) | (apart == cells - 1)), 1.0, 0.0).astype(jnp.bfloat16)


def section_kernel(number, chunk, halo, has_incoming, has_next, hands_on, n_saved, flags, offsets, kappa, forcing, *refs):
    refs = list(refs)
    incoming = refs.pop(0) if has_incoming else None
    upper, lower = refs.pop(0), refs.pop(0)
    following = refs.pop(0) if has_next else None
    weights = refs.pop(0)
    given = refs.pop(0) if hands_on else None
    saved = [] if has_next else [refs.pop(0) for _ in range(n_saved)]
    if has_next:
        own_out, up_out, down_out = refs.pop(0), refs.pop(0), refs.pop(0)
        passed, given_v = (refs.pop(0), refs.pop()) if hands_on else (None, None)
        k_v, once, smooth, own_v, up_s, down_s, pack_v, sems = refs
    else:
        if chunk:
            refs.pop(0)
        result, k_v, once, smooth, own_v, turned, sems = refs
    fields, cells = upper.shape[1:]
    rows = forcing.shape[0]
    count, per_row = weights.shape[:2]
    block = weights.shape[-1]
    extent = rows + 2 * halo
    lo, hi = halo, halo + rows

    if hands_on:
        @pl.when(flags[0] != number)
        def _():
            for copy in (
                pltpu.make_async_copy(given, given_v, sems.at[0]), pltpu.make_async_copy(given_v, passed, sems.at[1])
            ):
                copy.start()
                copy.wait()

    @pl.when(flags[0] == number)
    def _():
        mine = slice(chunk * fields, (chunk + 1) * fields)
        beside = beside_matrix(cells)
        top = jnp.where(flags[1] == 1, 0.0, 1.0)
        bottom = jnp.where(flags[2] == 1, 0.0, 1.0)
        for edge, start in ((upper, 0), (lower, hi)):
            parts = edge[halo].astype(jnp.float32)
            k_v[start:start + halo, :] = parts[:halo] + parts[halo:2 * halo] + parts[2 * halo:3 * halo]
        k_v[lo:hi, :] = kappa[...]

        def entry(i):
            if i < lo:
                return upper[i].astype(jnp.float32)
            if i >= hi:
                return lower[i - hi].astype(jnp.float32)
            value = forcing[i - lo, mine]
            if has_incoming:
                value = value + incoming[i - lo].astype(jnp.float32)
            return value

        def step(i, here, north, south, east_west):
            if i == lo:
                north = north * top
            if i == lo - 1:
                south = south * top
            if i == hi:
                north = north * bottom
            if i == hi - 1:
                south = south * bottom
            return here + k_v[i:i + 1, :] * ((north + south) + (east_west - 4.0 * here))

        def pair_beside(first, second):
            joined = jnp.concatenate([first.astype(jnp.bfloat16), second.astype(jnp.bfloat16)], axis=1)
            total = jnp.dot(joined, beside, preferred_element_type=jnp.float32)
            return total[:, :cells], total[:, cells:]

        there, after = None, entry(0)
        for i in range(0, extent, 2):
            before, here, there = there, after, entry(i + 1)
            after = entry(i + 2) if i + 2 < extent else None
            ew_here, ew_there = pair_beside(here, there)
            if i > 0:
                once[i] = step(i, here, before, there, ew_here)
            if i + 2 < extent:
                once[i + 1] = step(i + 1, there, here, after, ew_there)
        for i in range(2, extent - 2, 2):
            here, there = once[i], once[i + 1]
            ew_here, ew_there = pair_beside(here, there)
            out = i // 2 - 1
            smooth[out, :, :cells] = step(i, here, once[i - 1], there, ew_here).astype(jnp.bfloat16)
            smooth[out, :, cells:] = step(i + 1, there, here, once[i + 2], ew_there).astype(jnp.bfloat16)

        half = (halo - EDGE) * cells // block
        block_rows = block // cells
        stores = []
        if has_next:
            parts = following[rows].astype(jnp.float32)
            parts = [parts[p * rows:(p + 1) * rows] for p in range(3)]
            up_s[halo] = joined([part[:halo] for part in parts], pack_v)
            down_s[halo] = joined([part[rows - halo:] for part in parts], pack_v)
        for j in range(count):
            total = None
            for k in range(per_row):
                source = smooth[offsets[j, k] + (j + half)]
                term = lax.dot_general(
                    source, weights[j, k], (((1,), (1,)), ((), ())), preferred_element_type=jnp.float32
                )
                total = term if total is None else total + term
            for r in range(block_rows):
                row = j * block_rows + r
                value = total[:, r * cells:(r + 1) * cells].astype(jnp.bfloat16)
                own_v[row] = value
                if has_next:
                    entry_next = value.astype(jnp.float32) + following[row, mine].astype(jnp.float32)
                    if row < halo:
                        up_s[row] = entry_next.astype(jnp.bfloat16)
                    if row >= rows - halo:
                        down_s[row - (rows - halo)] = entry_next.astype(jnp.bfloat16)
                    if row == halo - 1:
                        stores.append(pltpu.make_async_copy(up_s, up_out, sems.at[0]))
                        stores[-1].start()
        if has_next:
            ends = [
                pltpu.make_async_copy(down_s, down_out, sems.at[1]),
                pltpu.make_async_copy(own_v, own_out, sems.at[2]),
            ]
            start_all(ends)
            wait_all(stores + ends)

    if not has_next:
        for i, kept in enumerate(saved):
            @pl.when(flags[0] == i)
            def _(kept=kept):
                copy = pltpu.make_async_copy(kept, own_v, sems.at[0])
                copy.start()
                copy.wait()

        lanes = 16
        for y in range(0, rows, lanes):
            turned[:, y:y + lanes, :] = jnp.swapaxes(own_v[y:y + lanes], 0, 1)
        copy = pltpu.make_async_copy(turned, result.at[pl.ds(chunk * fields, fields)], sems.at[1])
        copy.start()
        copy.wait()


def section(number, chunk, halo, flags, offsets, kappa, forcing, incoming, upper, lower, following, weights, given, saved, result):
    rows, total, cells = forcing.shape
    fields = upper.shape[1]
    count, per_row, block, _ = weights.shape
    has_incoming, has_next = incoming is not None, following is not None
    operands = [flags, offsets]
    forcing, weights = (pltpu.with_memory_space_constraint(value, pltpu.VMEM) for value in (forcing, weights))
    for value in (kappa, forcing, incoming, upper, lower, following, weights):
        if value is not None:
            operands.append(value)
    specs = [SMEM] * 2 + [VMEM] * (len(operands) - 2)
    if given is not None:
        operands.append(pltpu.with_memory_space_constraint(given, pltpu.HBM))
        specs.append(HBM)
    extent = rows + 2 * halo
    scratch = [
        pltpu.VMEM((extent, cells), jnp.float32),
        pltpu.VMEM((extent, fields, cells), jnp.float32),
        pltpu.VMEM(((extent - 2 * EDGE) * cells // block, fields, block), jnp.bfloat16),
        pltpu.VMEM((rows, fields, cells), jnp.bfloat16),
    ]
    aliases = {}
    if has_next:
        outs = [jax.ShapeDtypeStruct((n, fields, cells), jnp.bfloat16) for n in (rows, halo + 1, halo + 1)]
        if given is not None:
            outs.append(pltpu.HBM(given.shape, given.dtype))
        scratch += [pltpu.VMEM((halo + 1, fields, cells), jnp.bfloat16)] * 2 + [pltpu.VMEM((fields, cells), jnp.float32)]
    else:
        outs = [jax.ShapeDtypeStruct((total, rows, cells), jnp.bfloat16)]
        scratch += [pltpu.VMEM((fields, rows, cells), jnp.bfloat16)]
        operands += [pltpu.with_memory_space_constraint(value, pltpu.HBM) for value in saved]
        specs += [HBM] * len(saved)
        if result is not None:
            aliases = {len(operands): 0}
            operands.append(result)
            specs.append(HBM)
    return pl.pallas_call(
        functools.partial(section_kernel, number, chunk, halo, has_incoming, has_next, given is not None, len(saved)),
        in_specs=specs,
        out_shape=outs,
        out_specs=[ANY] * 3 + [HBM] * (len(outs) - 3) if has_next else [HBM],
        input_output_aliases=aliases,
        scratch_shapes=scratch + [pltpu.SemaphoreType.DMA((3,))] + (
            [pltpu.VMEM(given.shape, given.dtype)] if given is not None else []
        ),
        compiler_params=pltpu.CompilerParams(vmem_limit_bytes=LIMIT),
        cost_estimate=pl.CostEstimate(
            flops=FLOPS * 2 * count * per_row * block * block * fields, bytes_accessed=weights.size * 2, transcendentals=0,
        ),
    )(*operands)


def local(forcing, kappa, col_blocks, remap_weights):
    n_tile = lax.axis_size("tile")
    n_section = lax.axis_size("comp")
    tile_pos = lax.axis_index("tile")
    section_pos = lax.axis_index("comp")
    weights = remap_weights[0]
    count, block = weights.shape[0], weights.shape[-1]
    rows, cells = forcing.shape[-2:]
    half = count // 2
    halo = half * block // cells + EDGE
    total_blocks = count * n_tile
    global_block = tile_pos * count + jnp.arange(count, dtype=jnp.int32)
    offsets = jnp.mod(col_blocks[0] - global_block[:, None] + half, total_blocks) - half

    def place(s, t):
        return s * n_tile + t % n_tile

    def send(value, source, target, shift, swap=True):
        pairs = [(place(source, t), place(target, t + shift)) for t in range(n_tile)]
        others = [s for s in range(n_section) if s not in (source, target)]
        if swap and source == target:
            rest = list(zip(others, others[1:] + others[:1]))
        elif swap and source ^ 1 == target and n_section % 2 == 0:
            rest = [(target, source)] + [(s, s ^ 1) for s in others]
        else:
            rest = []
        pairs += [(place(s, t), place(to, t)) for s, to in rest for t in range(n_tile)]
        return lax.ppermute(value, AXES, pairs)

    fields = forcing.reshape(-1, rows, cells)
    flags = jnp.stack([section_pos, tile_pos == 0, tile_pos == n_tile - 1]).astype(jnp.int32)
    k_here = kappa[0]
    narrow, *edges = prepare(fields, k_here, halo)
    arrivals = []
    for c in range(CHUNKS):
        arrivals.append((None, send(edges[2 * c + 1], 0, 0, 1), send(edges[2 * c], 0, 0, -1)))
    weights, by_row = load(weights, fields, (flags, offsets))
    following = [lax.ppermute(narrow, "comp", [(s, s ^ 1) for s in range(n_section) if s ^ 1 < n_section])]
    owns = [[] for _ in range(CHUNKS)]
    result = None
    for s in range(n_section):
        last = s + 1 == n_section
        leaving = []
        for c in range(CHUNKS):
            incoming, upper, lower = arrivals[c]
            parts = section(
                s, c, halo, flags, offsets, k_here, by_row, incoming, upper, lower,
                None if last else following[s % 2], weights, narrow if s + c == 0 else None,
                owns[c] if last else [], result,
            )
            if last:
                result = parts[0]
            else:
                own, up, down, *passed = parts
                if passed:
                    following.append(lax.ppermute(passed[0], "comp", [(i + 1, i) for i in range(1, n_section - 1, 2)]))
                owns[c].append(own)
                sent = [send(part, s, s + 1, shift, c == 0) for part, shift in ((own, 0), (down, 1), (up, -1))]
                leaving.append(sent)
        arrivals = leaving
    return result.reshape(forcing.shape)


def solution(mesh):
    placed = (
        P("comp", None, None, "tile", None),
        P("comp", "tile", None),
        P("comp", "tile", None),
        P("comp", "tile", None, None, None),
    )
    return jax.shard_map(
        local,
        mesh=mesh,
        in_specs=placed,
        out_specs=P("comp", None, None, "tile", None),
        check_vma=False,
    )
```

```python
import functools

import jax
import jax.numpy as jnp
from jax import lax
from jax.experimental import pallas as pl
from jax.experimental.pallas import tpu as pltpu
from jax.sharding import PartitionSpec as P

AXES = ("comp", "tile")
SHARES = (1, 1)
EDGE = 2
LIMIT = 24 << 20
WEIGHT = 20
HBM = pl.BlockSpec(memory_space=pltpu.HBM)
VMEM = pl.BlockSpec(memory_space=pltpu.VMEM)
SMEM = pl.BlockSpec(memory_space=pltpu.SMEM)
ANY = pl.BlockSpec(memory_space=pl.ANY)


def start_all(copies):
    for copy in copies:
        copy.start()


def wait_all(copies):
    for copy in copies:
        copy.wait()


def in_hbm(value):
    return pltpu.with_memory_space_constraint(value, pltpu.HBM)


def in_vmem(value):
    return pltpu.with_memory_space_constraint(value, pltpu.VMEM)


def split(value):
    parts = []
    for _ in range(3):
        head = value.astype(jnp.bfloat16).astype(jnp.float32)
        parts.append(head)
        value = value - head
    return parts


def joined(parts, room):
    at = 0
    for part in parts:
        room[at:at + part.shape[0], :] = part
        at += part.shape[0]
    room[at:, :] = jnp.zeros((room.shape[0] - at, room.shape[1]), jnp.float32)
    return room[...].astype(jnp.bfloat16)


def prepare_kernel(flags, columns, forcing, kappa, *refs):
    offsets, by_row, narrow, again, first, last, c_v, f_v, k_v, pack, sems, k_sem, c_sem = refs
    total, rows, cells = f_v.shape
    halo = first.shape[0] - 1
    step = rows // sems.shape[0]
    loads = []
    for i in range(sems.shape[0]):
        part = pl.ds(i * step, step)
        loads.append(pltpu.make_async_copy(forcing.at[:, part], f_v.at[:, part], sems.at[i]))
    fetch = pltpu.make_async_copy(kappa, k_v, k_sem)
    take = pltpu.make_async_copy(columns, c_v, c_sem)
    take.start()
    fetch.start()
    start_all(loads)
    take.wait()
    count = columns.shape[1]
    ahead = c_v[...] - (flags[1] * count + lax.broadcasted_iota(jnp.int32, columns.shape, 1)) + count // 2
    every = flags[2] * count
    ahead = jnp.where(ahead < 0, ahead + every, jnp.where(ahead >= every, ahead - every, ahead))
    offsets[...] = ahead - count // 2
    fetch.wait()
    parts = split(k_v[...])
    narrow[rows] = joined(parts, pack)
    again[rows] = narrow[rows]
    first[halo] = joined([part[:halo] for part in parts], pack)
    last[halo] = joined([part[rows - halo:] for part in parts], pack)
    for i, load in enumerate(loads):
        load.wait()
        turned = jnp.swapaxes(f_v[:, i * step:(i + 1) * step, :], 0, 1)
        by_row[i * step:(i + 1) * step] = turned
        for r in range(step):
            y = i * step + r
            value = turned[r].astype(jnp.bfloat16)
            narrow[y] = value
            again[y] = value
            if y < halo:
                first[y] = value
            if y >= rows - halo:
                last[y - (rows - halo)] = value


def prepare(flags, columns, fields, kappa, halo):
    total, rows, cells = fields.shape
    return pl.pallas_call(
        prepare_kernel,
        in_specs=[SMEM, HBM, HBM, HBM],
        out_shape=[
            jax.ShapeDtypeStruct(columns.shape, columns.dtype),
            pltpu.VMEM((rows, total, cells), jnp.float32),
        ] + [jax.ShapeDtypeStruct((n + 1, total, cells), jnp.bfloat16) for n in (rows, rows, halo, halo)],
        out_specs=[VMEM] * 6,
        scratch_shapes=[
            pltpu.VMEM(columns.shape, columns.dtype),
            pltpu.VMEM((total, rows, cells), jnp.float32),
            pltpu.VMEM(kappa.shape, kappa.dtype),
            pltpu.VMEM((total, cells), jnp.float32),
            pltpu.SemaphoreType.DMA((rows // 8,)),
            pltpu.SemaphoreType.DMA,
            pltpu.SemaphoreType.DMA,
        ],
        compiler_params=pltpu.CompilerParams(vmem_limit_bytes=LIMIT),
        cost_estimate=pl.CostEstimate(flops=0, bytes_accessed=fields.size * 12, transcendentals=0),
    )(flags, in_hbm(columns), in_hbm(fields), in_hbm(kappa))


def load_kernel(flags, weights, *refs):
    held, sems = refs[-3], refs[-1]
    count, per_row = weights.shape[:2]
    loads = [pltpu.make_async_copy(weights.at[j], held.at[j], sems.at[j]) for j in range(count)]
    start_all(loads)
    wait_all(loads)

    @pl.when(flags[0] != 0)
    def _():
        def turn(i, _):
            j, k = i // per_row, i % per_row
            held[j, k] = held[j, k].T
            return 0

        lax.fori_loop(0, count * per_row, turn, 0, unroll=4)


def load(flags, weights, passed):
    return pl.pallas_call(
        load_kernel,
        in_specs=[SMEM, HBM, ANY],
        out_shape=[pltpu.VMEM(weights.shape, weights.dtype), jax.ShapeDtypeStruct(passed.shape, passed.dtype)],
        out_specs=[VMEM, ANY],
        input_output_aliases={2: 1},
        scratch_shapes=[pltpu.SemaphoreType.DMA((weights.shape[0],))],
        compiler_params=pltpu.CompilerParams(vmem_limit_bytes=LIMIT),
        cost_estimate=pl.CostEstimate(flops=0, bytes_accessed=weights.size * 4, transcendentals=0),
    )(flags, in_hbm(weights), passed)


def beside_matrix(cells):
    source = lax.broadcasted_iota(jnp.int32, (2 * cells, 2 * cells), 0)
    target = lax.broadcasted_iota(jnp.int32, (2 * cells, 2 * cells), 1)
    apart = (source - target + 2 * cells) % cells
    same = (source < cells) == (target < cells)
    return jnp.where(same & ((apart == 1) | (apart == cells - 1)), 1.0, 0.0).astype(jnp.bfloat16)


def section_kernel(number, bounds, halo, n_saved, has_next, flags, offsets, kappa, forcing, *refs):
    refs = list(refs)
    incoming = refs.pop(0) if number else None
    upper, lower = refs.pop(0), refs.pop(0)
    following = refs.pop(0) if has_next else None
    weights = refs.pop(0)
    saved = [refs.pop(0) for _ in range(n_saved)]
    if has_next:
        own_out, up_out, down_out = refs.pop(0), refs.pop(0), refs.pop(0)
    else:
        if bounds[0]:
            refs.pop(0)
        result = refs.pop(0)
    k_v, once, smooth, own_v, *rest, sems = refs
    rows, _, cells = forcing.shape
    fields = bounds[1] - bounds[0]
    count, per_row = weights.shape[:2]
    block = weights.shape[-1]
    extent = rows + 2 * halo
    lo, hi = halo, halo + rows

    @pl.when(flags[0] == number)
    def _():
        mine = slice(*bounds)
        theirs = slice(None) if number else mine
        beside = beside_matrix(cells)
        top = jnp.where(flags[1] == 0, 0.0, 1.0)
        bottom = jnp.where(flags[1] == flags[2] - 1, 0.0, 1.0)
        for edge, start in ((upper, 0), (lower, hi)):
            parts = edge[halo:].astype(jnp.float32).reshape(-1, cells)
            k_v[start:start + halo, :] = parts[:halo] + parts[halo:2 * halo] + parts[2 * halo:3 * halo]
        k_v[lo:hi, :] = kappa[...]

        def entry(i):
            if i < lo:
                return upper[i, theirs].astype(jnp.float32)
            if i >= hi:
                return lower[i - hi, theirs].astype(jnp.float32)
            value = forcing[i - lo, mine]
            if number:
                value = value + incoming[i - lo].astype(jnp.float32)
            return value

        def step(i, here, north, south, east_west):
            if i == lo:
                north = north * top
            if i == lo - 1:
                south = south * top
            if i == hi:
                north = north * bottom
            if i == hi - 1:
                south = south * bottom
            return here + k_v[i:i + 1, :] * ((north + south) + (east_west - 4.0 * here))

        def pair_beside(a, b):
            both = jnp.concatenate([a.astype(jnp.bfloat16), b.astype(jnp.bfloat16)], axis=1)
            total = jnp.dot(both, beside, preferred_element_type=jnp.float32)
            return total[:, :cells], total[:, cells:]

        there, after = None, entry(0)
        for i in range(0, extent, 2):
            before, here, there = there, after, entry(i + 1)
            after = entry(i + 2) if i + 2 < extent else None
            ew_here, ew_there = pair_beside(here, there)
            if i > 0:
                once[i] = step(i, here, before, there, ew_here)
            if i + 2 < extent:
                once[i + 1] = step(i + 1, there, here, after, ew_there)
        for i in range(2, extent - 2, 2):
            here, there = once[i], once[i + 1]
            ew_here, ew_there = pair_beside(here, there)
            out = i // 2 - 1
            smooth[out, :, :cells] = step(i, here, once[i - 1], there, ew_here).astype(jnp.bfloat16)
            smooth[out, :, cells:] = step(i + 1, there, here, once[i + 2], ew_there).astype(jnp.bfloat16)

        half = (halo - EDGE) * cells // block
        block_rows = block // cells
        stores = []
        if has_next:
            up_s, down_s, pack = rest
            parts = following[rows].astype(jnp.float32)
            parts = [parts[p * rows:(p + 1) * rows] for p in range(3)]
            tail = (up_s.shape[0] - halo, fields, cells)
            up_s[halo:] = joined([part[:halo] for part in parts], pack).reshape(tail)
            down_s[halo:] = joined([part[rows - halo:] for part in parts], pack).reshape(tail)
        for j in range(count):
            total = None
            for k in range(per_row):
                source = smooth[offsets[k, j] + (j + half)]
                term = lax.dot_general(
                    source, weights[j, k], (((1,), (0 if number else 1,)), ((), ())),
                    preferred_element_type=jnp.float32,
                )
                total = term if total is None else total + term
            for r in range(block_rows):
                row = j * block_rows + r
                value = total[:, r * cells:(r + 1) * cells].astype(jnp.bfloat16)
                own_v[row] = value
                if has_next:
                    entry_next = value.astype(jnp.float32) + following[row, mine].astype(jnp.float32)
                    if row < halo:
                        up_s[row] = entry_next.astype(jnp.bfloat16)
                    if row >= rows - halo:
                        down_s[row - (rows - halo)] = entry_next.astype(jnp.bfloat16)
                    if row == halo - 1:
                        stores.append(pltpu.make_async_copy(up_s, up_out, sems.at[0]))
                        stores[-1].start()
        if has_next:
            ends = [
                pltpu.make_async_copy(down_s, down_out, sems.at[1]),
                pltpu.make_async_copy(own_v, own_out, sems.at[2]),
            ]
            start_all(ends)
            wait_all(stores + ends)

    if not has_next:
        turned, = rest
        for i, kept in enumerate(saved):
            @pl.when(flags[0] == i)
            def _(kept=kept):
                copy = pltpu.make_async_copy(kept, own_v, sems.at[0])
                copy.start()
                copy.wait()

        step_rows = 16
        for y in range(0, rows, step_rows):
            turned[:, y:y + step_rows, :] = jnp.swapaxes(own_v[y:y + step_rows], 0, 1)
        copy = pltpu.make_async_copy(turned, result.at[pl.ds(bounds[0], fields)], sems.at[1])
        copy.start()
        copy.wait()


def section(number, bounds, halo, flags, offsets, kappa, forcing, arrived, following, weights, saved, result):
    rows, total, cells = forcing.shape
    fields = bounds[1] - bounds[0]
    count, per_row, block, _ = weights.shape
    has_next = following is not None
    operands = [flags, offsets, kappa, in_vmem(forcing)] + arrived
    if has_next:
        operands.append(following)
    specs = [SMEM] * 2 + [VMEM] * (len(operands) - 2)
    operands.append(in_vmem(weights))
    specs.append(VMEM)
    extent = rows + 2 * halo
    packed = -(-3 * halo // fields)
    scratch = [
        pltpu.VMEM((extent, cells), jnp.float32),
        pltpu.VMEM((extent, fields, cells), jnp.float32),
        pltpu.VMEM(((extent - 2 * EDGE) * cells // block, fields, block), jnp.bfloat16),
        pltpu.VMEM((rows, fields, cells), jnp.bfloat16),
    ]
    aliases = {}
    if has_next:
        outs = [jax.ShapeDtypeStruct((n, fields, cells), jnp.bfloat16) for n in (rows, halo + packed, halo + packed)]
        out_specs = [ANY] * 3
        scratch += [pltpu.VMEM((halo + packed, fields, cells), jnp.bfloat16)] * 2
        scratch.append(pltpu.VMEM((packed * fields, cells), jnp.float32))
    else:
        outs = [jax.ShapeDtypeStruct((total, rows, cells), jnp.bfloat16)]
        out_specs = [HBM]
        scratch += [pltpu.VMEM((fields, rows, cells), jnp.bfloat16)]
        operands += [in_hbm(value) for value in saved]
        specs += [HBM] * len(saved)
        if result is not None:
            aliases = {len(operands): 0}
            operands.append(result)
            specs.append(HBM)
    scratch.append(pltpu.SemaphoreType.DMA((3,)))
    return pl.pallas_call(
        functools.partial(section_kernel, number, bounds, halo, len(saved), has_next),
        in_specs=specs,
        out_shape=outs,
        out_specs=out_specs,
        input_output_aliases=aliases,
        scratch_shapes=scratch,
        compiler_params=pltpu.CompilerParams(vmem_limit_bytes=LIMIT),
        cost_estimate=pl.CostEstimate(
            flops=WEIGHT * 2 * count * per_row * block * block * fields, bytes_accessed=weights.size * 2, transcendentals=0
        ),
    )(*operands)


def local(forcing, kappa, col_blocks, remap_weights):
    n_tile = lax.axis_size("tile")
    n_section = lax.axis_size("comp")
    tile_pos = lax.axis_index("tile")
    section_pos = lax.axis_index("comp")
    weights = remap_weights[0]
    count, block = weights.shape[0], weights.shape[-1]
    rows, cells = forcing.shape[-2:]
    half = count // 2
    halo = half * block // cells + EDGE
    flags = jnp.stack([section_pos, tile_pos, jnp.full_like(tile_pos, n_tile)]).astype(jnp.int32)

    def place(s, t):
        return s * n_tile + t % n_tile

    def send(value, source, target, shift):
        pairs = [(place(source, t), place(target, t + shift)) for t in range(n_tile)]
        others = [s for s in range(n_section) if s not in (source, target)]
        if source == target:
            rest = list(zip(others, others[1:] + others[:1]))
        elif source ^ 1 == target and n_section % 2 == 0:
            rest = [(target, source)] + [(s, s ^ 1) for s in others]
        else:
            rest = []
        pairs += [(place(s, t), place(to, t)) for s, to in rest for t in range(n_tile)]
        return lax.ppermute(value, AXES, pairs)

    offsets, by_row, narrow, again, first, last = prepare(
        flags, col_blocks[0].T, forcing.reshape(-1, rows, cells), kappa[0], halo
    )
    total = by_row.shape[1]
    marks = [total * sum(SHARES[:c]) // sum(SHARES) for c in range(len(SHARES) + 1)]
    chunks = list(zip(marks[:-1], marks[1:]))
    arrivals = [[send(last, 0, 0, 1), send(first, 0, 0, -1)]] * len(chunks)
    weights, again = load(flags, weights, again)
    following = [
        lax.ppermute(narrow, "comp", [(s, s ^ 1) for s in range(n_section) if s ^ 1 < n_section]),
        lax.ppermute(again, "comp", [(s + 1, s) for s in range(1, n_section - 1, 2)]),
    ]
    owns = [[] for _ in chunks]
    result = None
    for s in range(n_section):
        last = s + 1 == n_section
        leaving = []
        for c, bounds in enumerate(chunks):
            parts = section(
                s, bounds, halo, flags, offsets, kappa[0], by_row, arrivals[c], None if last else following[s % 2],
                weights, owns[c] if last else [], result,
            )
            if last:
                result = parts[0]
                continue
            own, up, down = parts
            owns[c].append(own)
            leaving.append([send(part, s, s + 1, shift) for part, shift in ((own, 0), (down, 1), (up, -1))])
        arrivals = leaving
    return result.reshape(forcing.shape)


def solution(mesh):
    placed = (
        P("comp", None, None, "tile", None),
        P("comp", "tile", None),
        P("comp", "tile", None),
        P("comp", "tile", None, None, None),
    )
    return jax.shard_map(
        local,
        mesh=mesh,
        in_specs=placed,
        out_specs=P("comp", None, None, "tile", None),
        check_vma=False,
    )
```

```python
import functools

import jax
import jax.numpy as jnp
from jax import lax
from jax.experimental import pallas as pl
from jax.experimental.pallas import tpu as pltpu
from jax.sharding import PartitionSpec as P

AXES = ("comp", "tile")
SHARES = (1, 1)
EDGE = 2
LIMIT = 24 << 20
WEIGHT = 20
HBM = pl.BlockSpec(memory_space=pltpu.HBM)
VMEM = pl.BlockSpec(memory_space=pltpu.VMEM)
SMEM = pl.BlockSpec(memory_space=pltpu.SMEM)
ANY = pl.BlockSpec(memory_space=pl.ANY)


def start_all(copies):
    for copy in copies:
        copy.start()


def wait_all(copies):
    for copy in copies:
        copy.wait()


def in_hbm(value):
    return pltpu.with_memory_space_constraint(value, pltpu.HBM)


def in_vmem(value):
    return pltpu.with_memory_space_constraint(value, pltpu.VMEM)


def split(value):
    parts = []
    for _ in range(3):
        head = value.astype(jnp.bfloat16).astype(jnp.float32)
        parts.append(head)
        value = value - head
    return parts


def joined(parts, room):
    at = 0
    for part in parts:
        room[at:at + part.shape[0], :] = part
        at += part.shape[0]
    room[at:, :] = jnp.zeros((room.shape[0] - at, room.shape[1]), jnp.float32)
    return room[...].astype(jnp.bfloat16)


def prepare_kernel(halo, marks, flags, columns, forcing, kappa, *refs):
    offsets, by_row, narrow, *edges, c_v, f_v, k_v, pack, sems, k_sem, c_sem = refs
    total, rows, cells = f_v.shape
    step = rows // sems.shape[0]
    loads = []
    for i in range(sems.shape[0]):
        part = pl.ds(i * step, step)
        loads.append(pltpu.make_async_copy(forcing.at[:, part], f_v.at[:, part], sems.at[i]))
    fetch = pltpu.make_async_copy(kappa, k_v, k_sem)
    take = pltpu.make_async_copy(columns, c_v, c_sem)
    take.start()
    fetch.start()
    start_all(loads)
    take.wait()
    count = columns.shape[1]
    ahead = c_v[...] - (flags[1] * count + lax.broadcasted_iota(jnp.int32, columns.shape, 1)) + count // 2
    every = flags[2] * count
    ahead = jnp.where(ahead < 0, ahead + every, jnp.where(ahead >= every, ahead - every, ahead))
    offsets[...] = ahead - count // 2
    fetch.wait()
    parts = split(k_v[...])
    narrow[rows] = joined(parts, pack)
    for e, start in enumerate((0, rows - halo)):
        row = joined([part[start:start + halo] for part in parts], pack)
        for edge in edges[e::2]:
            tail = (edge.shape[0] - halo, *edge.shape[1:])
            edge[halo:] = row[:tail[0] * tail[1]].reshape(tail)
    for i, load in enumerate(loads):
        load.wait()
        turned = jnp.swapaxes(f_v[:, i * step:(i + 1) * step, :], 0, 1)
        by_row[i * step:(i + 1) * step] = turned
        for r in range(step):
            y = i * step + r
            value = turned[r].astype(jnp.bfloat16)
            narrow[y] = value
            for edge_first, edge_last, start, stop in zip(edges[0::2], edges[1::2], marks[:-1], marks[1:]):
                if y < halo:
                    edge_first[y] = value[start:stop]
                if y >= rows - halo:
                    edge_last[y - (rows - halo)] = value[start:stop]


def prepare(flags, columns, fields, kappa, halo, marks):
    edges = [
        jax.ShapeDtypeStruct((halo - (-3 * halo // (stop - start)), stop - start, kappa.shape[1]), jnp.bfloat16)
        for start, stop in zip(marks[:-1], marks[1:]) for _ in range(2)
    ]
    total, rows, cells = fields.shape
    return pl.pallas_call(
        functools.partial(prepare_kernel, halo, marks),
        in_specs=[SMEM, HBM, HBM, HBM],
        out_shape=[
            jax.ShapeDtypeStruct(columns.shape, columns.dtype),
            pltpu.VMEM((rows, total, cells), jnp.float32),
            jax.ShapeDtypeStruct((rows + 1, total, cells), jnp.bfloat16),
        ] + edges,
        out_specs=[VMEM] * (3 + len(edges)),
        scratch_shapes=[
            pltpu.VMEM(columns.shape, columns.dtype),
            pltpu.VMEM((total, rows, cells), jnp.float32),
            pltpu.VMEM(kappa.shape, kappa.dtype),
            pltpu.VMEM((total, cells), jnp.float32),
            pltpu.SemaphoreType.DMA((rows // 8,)),
            pltpu.SemaphoreType.DMA,
            pltpu.SemaphoreType.DMA,
        ],
        compiler_params=pltpu.CompilerParams(vmem_limit_bytes=LIMIT),
        cost_estimate=pl.CostEstimate(flops=0, bytes_accessed=fields.size * 12, transcendentals=0),
    )(flags, in_hbm(columns), in_hbm(fields), in_hbm(kappa))


def load_kernel(n_passed, flags, weights, *refs):
    held, sems = refs[n_passed], refs[-1]
    count, per_row = weights.shape[:2]
    loads = [pltpu.make_async_copy(weights.at[j], held.at[j], sems.at[j]) for j in range(count)]
    start_all(loads)
    wait_all(loads)

    @pl.when(flags[0] != 0)
    def _():
        def turn(i, _):
            j, k = i // per_row, i % per_row
            held[j, k] = held[j, k].T
            return 0

        lax.fori_loop(0, count * per_row, turn, 0, unroll=4)


def load(flags, weights, passed):
    return pl.pallas_call(
        functools.partial(load_kernel, len(passed)),
        in_specs=[SMEM, HBM] + [ANY] * len(passed),
        out_shape=[pltpu.VMEM(weights.shape, weights.dtype)] + [jax.ShapeDtypeStruct(p.shape, p.dtype) for p in passed],
        out_specs=[VMEM] + [ANY] * len(passed),
        input_output_aliases={2 + i: 1 + i for i in range(len(passed))},
        scratch_shapes=[pltpu.SemaphoreType.DMA((weights.shape[0],))],
        compiler_params=pltpu.CompilerParams(vmem_limit_bytes=LIMIT),
        cost_estimate=pl.CostEstimate(flops=0, bytes_accessed=weights.size * 4, transcendentals=0),
    )(flags, in_hbm(weights), *passed)


def beside_matrix(cells):
    source = lax.broadcasted_iota(jnp.int32, (2 * cells, 2 * cells), 0)
    target = lax.broadcasted_iota(jnp.int32, (2 * cells, 2 * cells), 1)
    apart = (source - target + 2 * cells) % cells
    same = (source < cells) == (target < cells)
    return jnp.where(same & ((apart == 1) | (apart == cells - 1)), 1.0, 0.0).astype(jnp.bfloat16)


def section_kernel(turned_edges, number, bounds, halo, n_saved, has_next, flags, offsets, kappa, forcing, *refs):
    refs = list(refs)
    incoming = refs.pop(0) if number else None
    upper, lower = refs.pop(0), refs.pop(0)
    if turned_edges:
        upper, lower = lower, upper
    ahead = [refs.pop(0) for _ in range(2 if number else 1)] if has_next else []
    weights = refs.pop(0)
    saved = [refs.pop(0) for _ in range(n_saved)]
    if has_next:
        own_out, up_out, down_out = refs.pop(0), refs.pop(0), refs.pop(0)
    else:
        if bounds[0]:
            refs.pop(0)
        result = refs.pop(0)
    if has_next:
        k_v, once, smooth, pack = refs
        own_v, up_s, down_s = own_out, up_out, down_out
    else:
        k_v, once, smooth, own_v, turned, sems = refs
    rows, _, cells = forcing.shape
    fields = bounds[1] - bounds[0]
    count, per_row = weights.shape[:2]
    block = weights.shape[-1]
    extent = rows + 2 * halo
    lo, hi = halo, halo + rows

    @pl.when(flags[0] == number)
    def _():
        mine = slice(*bounds)
        beside = beside_matrix(cells)
        top = jnp.where(flags[1] == 0, 0.0, 1.0)
        bottom = jnp.where(flags[1] == flags[2] - 1, 0.0, 1.0)
        for edge, start in ((upper, 0), (lower, hi)):
            parts = edge[halo:].astype(jnp.float32).reshape(-1, cells)
            k_v[start:start + halo, :] = parts[:halo] + parts[halo:2 * halo] + parts[2 * halo:3 * halo]
        k_v[lo:hi, :] = kappa[...]

        def entry(i):
            if i < lo:
                return upper[i].astype(jnp.float32)
            if i >= hi:
                return lower[i - hi].astype(jnp.float32)
            value = forcing[i - lo, mine]
            if number:
                value = value + incoming[i - lo].astype(jnp.float32)
            return value

        def step(i, here, north, south, east_west):
            if i == lo:
                north = north * top
            if i == lo - 1:
                south = south * top
            if i == hi:
                north = north * bottom
            if i == hi - 1:
                south = south * bottom
            return here + k_v[i:i + 1, :] * ((north + south) + (east_west - 4.0 * here))

        def pair_beside(a, b):
            both = jnp.concatenate([a.astype(jnp.bfloat16), b.astype(jnp.bfloat16)], axis=1)
            total = jnp.dot(both, beside, preferred_element_type=jnp.float32)
            return total[:, :cells], total[:, cells:]

        there, after = None, entry(0)
        for i in range(0, extent, 2):
            before, here, there = there, after, entry(i + 1)
            after = entry(i + 2) if i + 2 < extent else None
            ew_here, ew_there = pair_beside(here, there)
            if i > 0:
                once[i] = step(i, here, before, there, ew_here)
            if i + 2 < extent:
                once[i + 1] = step(i + 1, there, here, after, ew_there)
        for i in range(2, extent - 2, 2):
            here, there = once[i], once[i + 1]
            ew_here, ew_there = pair_beside(here, there)
            out = i // 2 - 1
            smooth[out, :, :cells] = step(i, here, once[i - 1], there, ew_here).astype(jnp.bfloat16)
            smooth[out, :, cells:] = step(i + 1, there, here, once[i + 2], ew_there).astype(jnp.bfloat16)

        half = (halo - EDGE) * cells // block
        block_rows = block // cells
        if has_next:
            if number:
                up_s[halo:] = ahead[0][halo:]
                down_s[halo:] = ahead[1][halo:]
            else:
                parts = ahead[0][rows].astype(jnp.float32)
                parts = [parts[p * rows:(p + 1) * rows] for p in range(3)]
                tail = (up_s.shape[0] - halo, fields, cells)
                up_s[halo:] = joined([part[:halo] for part in parts], pack).reshape(tail)
                down_s[halo:] = joined([part[rows - halo:] for part in parts], pack).reshape(tail)
        for j in range(count):
            total = None
            for k in range(per_row):
                source = smooth[offsets[k, j] + (j + half)]
                term = lax.dot_general(
                    source, weights[j, k], (((1,), (0 if number else 1,)), ((), ())),
                    preferred_element_type=jnp.float32,
                )
                total = term if total is None else total + term
            for r in range(block_rows):
                row = j * block_rows + r
                value = total[:, r * cells:(r + 1) * cells].astype(jnp.bfloat16)
                own_v[row] = value
                if has_next:
                    if number:
                        ahead_row = ahead[0][row] if row < halo else ahead[1][row - (rows - halo)]
                    else:
                        ahead_row = ahead[0][row, mine]
                    entry_next = value.astype(jnp.float32) + ahead_row.astype(jnp.float32)
                    if row < halo:
                        up_s[row] = entry_next.astype(jnp.bfloat16)
                    if row >= rows - halo:
                        down_s[row - (rows - halo)] = entry_next.astype(jnp.bfloat16)

    if not has_next:
        for i, kept in enumerate(saved):
            @pl.when(flags[0] == i)
            def _(kept=kept):
                copy = pltpu.make_async_copy(kept, own_v, sems.at[0])
                copy.start()
                copy.wait()

        step_rows = 16
        for y in range(0, rows, step_rows):
            turned[:, y:y + step_rows, :] = jnp.swapaxes(own_v[y:y + step_rows], 0, 1)
        copy = pltpu.make_async_copy(turned, result.at[pl.ds(bounds[0], fields)], sems.at[1])
        copy.start()
        copy.wait()


def section(number, bounds, halo, flags, offsets, kappa, forcing, arrived, following, weights, saved, result):
    rows, total, cells = forcing.shape
    fields = bounds[1] - bounds[0]
    count, per_row, block, _ = weights.shape
    has_next = bool(following)
    turned_edges = number == 0 and bounds[0] > 0
    if turned_edges:
        arrived = arrived[::-1]
    operands = [flags, offsets, kappa, in_vmem(forcing)] + arrived
    operands += following
    specs = [SMEM] * 2 + [VMEM] * (len(operands) - 2)
    operands.append(in_vmem(weights))
    specs.append(VMEM)
    extent = rows + 2 * halo
    packed = -(-3 * halo // fields)
    scratch = [
        pltpu.VMEM((extent, cells), jnp.float32),
        pltpu.VMEM((extent, fields, cells), jnp.float32),
        pltpu.VMEM(((extent - 2 * EDGE) * cells // block, fields, block), jnp.bfloat16),
    ]
    aliases = {}
    if has_next:
        outs = [jax.ShapeDtypeStruct((n, fields, cells), jnp.bfloat16) for n in (rows, halo + packed, halo + packed)]
        out_specs = [VMEM] * 3
        scratch.append(pltpu.VMEM((packed * fields, cells), jnp.float32))
    else:
        outs = [jax.ShapeDtypeStruct((total, rows, cells), jnp.bfloat16)]
        out_specs = [HBM]
        scratch += [
            pltpu.VMEM((rows, fields, cells), jnp.bfloat16),
            pltpu.VMEM((fields, rows, cells), jnp.bfloat16),
            pltpu.SemaphoreType.DMA((2,)),
        ]
        operands += [in_hbm(value) for value in saved]
        specs += [HBM] * len(saved)
        if result is not None:
            aliases = {len(operands): 0}
            operands.append(result)
            specs.append(HBM)
    return pl.pallas_call(
        functools.partial(section_kernel, turned_edges, number, bounds, halo, len(saved), has_next),
        in_specs=specs,
        out_shape=outs,
        out_specs=out_specs,
        input_output_aliases=aliases,
        scratch_shapes=scratch,
        compiler_params=pltpu.CompilerParams(vmem_limit_bytes=LIMIT),
        cost_estimate=pl.CostEstimate(
            flops=WEIGHT * 2 * count * per_row * block * block * fields, bytes_accessed=weights.size * 2, transcendentals=0
        ),
    )(*operands)


def local(forcing, kappa, col_blocks, remap_weights):
    n_tile = lax.axis_size("tile")
    n_section = lax.axis_size("comp")
    tile_pos = lax.axis_index("tile")
    section_pos = lax.axis_index("comp")
    weights = remap_weights[0]
    count, block = weights.shape[0], weights.shape[-1]
    rows, cells = forcing.shape[-2:]
    half = count // 2
    halo = half * block // cells + EDGE
    flags = jnp.stack([section_pos, tile_pos, jnp.full_like(tile_pos, n_tile)]).astype(jnp.int32)

    def place(s, t):
        return s * n_tile + t % n_tile

    def send(value, source, target, shift):
        pairs = [(place(source, t), place(target, t + shift)) for t in range(n_tile)]
        others = [s for s in range(n_section) if s not in (source, target)]
        if source == target:
            rest = list(zip(others[1:] + others[:1], others))
        elif source ^ 1 == target and n_section % 2 == 0:
            rest = [(target, source)] + [(s, s ^ 1) for s in others]
        else:
            rest = []
        pairs += [(place(s, t), place(to, t)) for s, to in rest for t in range(n_tile)]
        return lax.ppermute(value, AXES, pairs)

    fields = forcing.reshape(-1, rows, cells)
    marks = [fields.shape[0] * sum(SHARES[:c]) // sum(SHARES) for c in range(len(SHARES) + 1)]
    offsets, by_row, narrow, *edges = prepare(flags, col_blocks[0].T, fields, kappa[0], halo, marks)
    weights, *edges[2:] = load(flags, weights, edges[2:])
    arrivals = []
    for c in range(len(SHARES)):
        sends = [(edges[2 * c + 1], 1), (edges[2 * c], -1)][::1 - c % 2 * 2]
        arrivals.append([send(edge, 0, 0, shift) for edge, shift in sends][::1 - c % 2 * 2])
    narrow = lax.ppermute(narrow, "comp", [(s, s ^ 1) for s in range(n_section) if s ^ 1 < n_section])
    following = [[[narrow]] * len(SHARES)] + [[pair[::-1] for pair in arrivals]] * (n_section - 2) + [[[]] * len(SHARES)]
    owns = [[] for _ in SHARES]
    result = None
    for s in range(n_section):
        last = s + 1 == n_section
        leaving = []
        for c, bounds in enumerate(zip(marks[:-1], marks[1:])):
            parts = section(
                s, bounds, halo, flags, offsets, kappa[0], by_row, arrivals[c], following[s][c],
                weights, owns[c] if last else [], result,
            )
            if last:
                result = parts[0]
                continue
            own, up, down = parts
            owns[c].append(own)
            leaving.append([send(part, s, s + 1, shift) for part, shift in ((own, 0), (down, 1), (up, -1))])
        arrivals = leaving
    return result.reshape(forcing.shape)


def solution(mesh):
    placed = (
        P("comp", None, None, "tile", None),
        P("comp", "tile", None),
        P("comp", "tile", None),
        P("comp", "tile", None, None, None),
    )
    return jax.shard_map(
        local,
        mesh=mesh,
        in_specs=placed,
        out_specs=P("comp", None, None, "tile", None),
        check_vma=False,
    )
```

```python
import functools

import jax
import jax.numpy as jnp
from jax import lax
from jax.experimental import pallas as pl
from jax.experimental.pallas import tpu as pltpu
from jax.sharding import PartitionSpec as P

AXES = ("comp", "tile")
SHARES = (1, 1)
EDGE = 2
LIMIT = 24 << 20
ORDERS = (((-2, -1), (-1, -2)), ((-1, -2, 0), (-1, -2, 0)))
WEIGHT = 20
HBM = pl.BlockSpec(memory_space=pltpu.HBM)
VMEM = pl.BlockSpec(memory_space=pltpu.VMEM)
SMEM = pl.BlockSpec(memory_space=pltpu.SMEM)
ANY = pl.BlockSpec(memory_space=pl.ANY)


def start_all(copies):
    for copy in copies:
        copy.start()


def wait_all(copies):
    for copy in copies:
        copy.wait()


def in_hbm(value):
    return pltpu.with_memory_space_constraint(value, pltpu.HBM)


def in_vmem(value):
    return pltpu.with_memory_space_constraint(value, pltpu.VMEM)


def split(value):
    parts = []
    for _ in range(3):
        head = value.astype(jnp.bfloat16).astype(jnp.float32)
        parts.append(head)
        value = value - head
    return parts


def packed_rows(halo, start, stop):
    return 0 if start else -(-3 * halo // (stop - start))


def joined(parts, room):
    at = 0
    for part in parts:
        room[at:at + part.shape[0], :] = part
        at += part.shape[0]
    room[at:, :] = jnp.zeros((room.shape[0] - at, room.shape[1]), jnp.float32)
    return room[...].astype(jnp.bfloat16)


def prepare_kernel(halo, marks, flags, columns, forcing, kappa, *refs):
    offsets, by_row, narrow, *edges, c_v, f_v, k_v, pack, sems, k_sem, c_sem = refs
    total, rows, cells = f_v.shape
    step = rows // sems.shape[0]
    loads = []
    for i in range(sems.shape[0]):
        part = pl.ds(i * step, step)
        loads.append(pltpu.make_async_copy(forcing.at[:, part], f_v.at[:, part], sems.at[i]))
    fetch = pltpu.make_async_copy(kappa, k_v, k_sem)
    take = pltpu.make_async_copy(columns, c_v, c_sem)
    take.start()
    fetch.start()
    start_all(loads)
    take.wait()
    count = columns.shape[1]
    ahead = c_v[...] - (flags[1] * count + lax.broadcasted_iota(jnp.int32, columns.shape, 1)) + count // 2
    every = flags[2] * count
    ahead = jnp.where(ahead < 0, ahead + every, jnp.where(ahead >= every, ahead - every, ahead))
    offsets[...] = ahead - count // 2
    fetch.wait()
    parts = split(k_v[...])
    narrow[rows] = joined(parts, pack)
    for e, start in enumerate((0, rows - halo)):
        row = joined([part[start:start + halo] for part in parts], pack)
        tail = (edges[e].shape[0] - halo, *edges[e].shape[1:])
        edges[e][halo:] = row[:tail[0] * tail[1]].reshape(tail)
    for i, load in enumerate(loads):
        load.wait()
        turned = jnp.swapaxes(f_v[:, i * step:(i + 1) * step, :], 0, 1)
        by_row[i * step:(i + 1) * step] = turned
        for r in range(step):
            y = i * step + r
            value = turned[r].astype(jnp.bfloat16)
            narrow[y] = value
            for edge_first, edge_last, start, stop in zip(edges[0::2], edges[1::2], marks[:-1], marks[1:]):
                if y < halo:
                    edge_first[y] = value[start:stop]
                if y >= rows - halo:
                    edge_last[y - (rows - halo)] = value[start:stop]


def prepare(flags, columns, fields, kappa, halo, marks):
    edges = [
        jax.ShapeDtypeStruct((halo + packed_rows(halo, 0, stop - start), stop - start, kappa.shape[1]), jnp.bfloat16)
        for start, stop in zip(marks[:-1], marks[1:]) for _ in range(2)
    ]
    total, rows, cells = fields.shape
    return pl.pallas_call(
        functools.partial(prepare_kernel, halo, marks),
        in_specs=[SMEM, HBM, HBM, HBM],
        out_shape=[
            jax.ShapeDtypeStruct(columns.shape, columns.dtype),
            pltpu.VMEM((rows, total, cells), jnp.float32),
            jax.ShapeDtypeStruct((rows + 1, total, cells), jnp.bfloat16),
        ] + edges,
        out_specs=[VMEM] * (3 + len(edges)),
        scratch_shapes=[
            pltpu.VMEM(columns.shape, columns.dtype),
            pltpu.VMEM((total, rows, cells), jnp.float32),
            pltpu.VMEM(kappa.shape, kappa.dtype),
            pltpu.VMEM((total, cells), jnp.float32),
            pltpu.SemaphoreType.DMA((rows // 8,)),
            pltpu.SemaphoreType.DMA,
            pltpu.SemaphoreType.DMA,
        ],
        compiler_params=pltpu.CompilerParams(vmem_limit_bytes=LIMIT),
        cost_estimate=pl.CostEstimate(flops=0, bytes_accessed=fields.size * 12, transcendentals=0),
    )(flags, in_hbm(columns), in_hbm(fields), in_hbm(kappa))


def load_kernel(n_passed, flags, weights, *refs):
    held, sems = refs[n_passed], refs[-1]
    count, per_row = weights.shape[:2]
    loads = [pltpu.make_async_copy(weights.at[j], held.at[j], sems.at[j]) for j in range(count)]
    start_all(loads)
    wait_all(loads)

    @pl.when(flags[0] != 0)
    def _():
        def turn(i, _):
            j, k = i // per_row, i % per_row
            held[j, k] = held[j, k].T
            return 0

        lax.fori_loop(0, count * per_row, turn, 0, unroll=4)


def load(flags, weights, passed):
    return pl.pallas_call(
        functools.partial(load_kernel, len(passed)),
        in_specs=[SMEM, HBM] + [ANY] * len(passed),
        out_shape=[pltpu.VMEM(weights.shape, weights.dtype)] + [jax.ShapeDtypeStruct(p.shape, p.dtype) for p in passed],
        out_specs=[VMEM] + [ANY] * len(passed),
        input_output_aliases={2 + i: 1 + i for i in range(len(passed))},
        scratch_shapes=[pltpu.SemaphoreType.DMA((weights.shape[0],))],
        compiler_params=pltpu.CompilerParams(vmem_limit_bytes=LIMIT),
        cost_estimate=pl.CostEstimate(flops=0, bytes_accessed=weights.size * 4, transcendentals=0),
    )(flags, in_hbm(weights), *passed)


def beside_matrix(cells):
    source = lax.broadcasted_iota(jnp.int32, (2 * cells, 2 * cells), 0)
    target = lax.broadcasted_iota(jnp.int32, (2 * cells, 2 * cells), 1)
    apart = (source - target + 2 * cells) % cells
    same = (source < cells) == (target < cells)
    return jnp.where(same & ((apart == 1) | (apart == cells - 1)), 1.0, 0.0).astype(jnp.bfloat16)


def section_kernel(order, number, bounds, halo, n_saved, has_next, flags, offsets, kappa, forcing, *refs):
    refs = list(refs)
    arrived = dict(zip(order, (refs.pop(0) for _ in order)))
    upper, lower, incoming = arrived[-2], arrived[-1], arrived.get(0)
    start_chunk = bounds[0] == 0
    ahead = [refs.pop(0) for _ in range(2 if number else 1)] if has_next else []
    weights = refs.pop(0)
    saved = [refs.pop(0) for _ in range(n_saved)]
    if has_next:
        own_out, up_out, down_out = refs.pop(0), refs.pop(0), refs.pop(0)
    else:
        if bounds[0]:
            refs.pop(0)
        result = refs.pop(0)
    if has_next:
        own_v, up_s, down_s = own_out, up_out, down_out
    k_v = refs.pop(0) if start_chunk else kappa
    once, smooth, *rest = refs
    if not has_next:
        own_v, turned, sems = rest
    rows, _, cells = forcing.shape
    fields = bounds[1] - bounds[0]
    count, per_row = weights.shape[:2]
    block = weights.shape[-1]
    extent = rows + 2 * halo
    lo, hi = halo, halo + rows

    if not has_next:
        part = rows // 2
        stores = [
            pltpu.make_async_copy(
                turned.at[:, pl.ds(i * part, part)], result.at[pl.ds(bounds[0], fields), pl.ds(i * part, part)], sems.at[i]
            )
            for i in range(2)
        ]

        def store(i):
            turned[:, i * part:(i + 1) * part, :] = jnp.swapaxes(own_v[i * part:(i + 1) * part], 0, 1)
            stores[i].start()

    @pl.when(flags[0] == number)
    def _():
        mine = slice(*bounds)
        beside = beside_matrix(cells)
        top = jnp.where(flags[1] == 0, 0.0, 1.0)
        bottom = jnp.where(flags[1] == flags[2] - 1, 0.0, 1.0)
        if start_chunk:
            for edge, start in ((upper, 0), (lower, hi)):
                parts = edge[halo:].astype(jnp.float32).reshape(-1, cells)
                k_v[start:start + halo, :] = parts[:halo] + parts[halo:2 * halo] + parts[2 * halo:3 * halo]
            k_v[lo:hi, :] = kappa[...]

        def entry(i):
            if i < lo:
                return upper[i].astype(jnp.float32)
            if i >= hi:
                return lower[i - hi].astype(jnp.float32)
            value = forcing[i - lo, mine]
            if number:
                value = value + incoming[i - lo].astype(jnp.float32)
            return value

        def step(i, here, north, south, east_west):
            if i == lo:
                north = north * top
            if i == lo - 1:
                south = south * top
            if i == hi:
                north = north * bottom
            if i == hi - 1:
                south = south * bottom
            return here + k_v[i:i + 1, :] * ((north + south) + (east_west - 4.0 * here))

        def pair_beside(a, b):
            both = jnp.concatenate([a.astype(jnp.bfloat16), b.astype(jnp.bfloat16)], axis=1)
            total = jnp.dot(both, beside, preferred_element_type=jnp.float32)
            return total[:, :cells], total[:, cells:]

        there, after = None, entry(0)
        for i in range(0, extent, 2):
            before, here, there = there, after, entry(i + 1)
            after = entry(i + 2) if i + 2 < extent else None
            ew_here, ew_there = pair_beside(here, there)
            if i > 0:
                once[i] = step(i, here, before, there, ew_here)
            if i + 2 < extent:
                once[i + 1] = step(i + 1, there, here, after, ew_there)
        for i in range(2, extent - 2, 2):
            here, there = once[i], once[i + 1]
            ew_here, ew_there = pair_beside(here, there)
            out = i // 2 - 1
            smooth[out, :, :cells] = step(i, here, once[i - 1], there, ew_here).astype(jnp.bfloat16)
            smooth[out, :, cells:] = step(i + 1, there, here, once[i + 2], ew_there).astype(jnp.bfloat16)

        half = (halo - EDGE) * cells // block
        block_rows = block // cells
        if has_next and start_chunk:
            pack, = rest
            if number:
                up_s[halo:] = ahead[0][halo:]
                down_s[halo:] = ahead[1][halo:]
            else:
                parts = ahead[0][rows].astype(jnp.float32)
                parts = [parts[p * rows:(p + 1) * rows] for p in range(3)]
                tail = (up_s.shape[0] - halo, fields, cells)
                up_s[halo:] = joined([part[:halo] for part in parts], pack).reshape(tail)
                down_s[halo:] = joined([part[rows - halo:] for part in parts], pack).reshape(tail)
        for j in range(count):
            total = None
            for k in range(per_row):
                source = smooth[offsets[k, j] + (j + half)]
                term = lax.dot_general(
                    source, weights[j, k], (((1,), (0 if number else 1,)), ((), ())),
                    preferred_element_type=jnp.float32,
                )
                total = term if total is None else total + term
            for r in range(block_rows):
                row = j * block_rows + r
                value = total[:, r * cells:(r + 1) * cells].astype(jnp.bfloat16)
                own_v[row] = value
                if has_next:
                    if number:
                        ahead_row = ahead[0][row] if row < halo else ahead[1][row - (rows - halo)]
                    else:
                        ahead_row = ahead[0][row, mine]
                    entry_next = value.astype(jnp.float32) + ahead_row.astype(jnp.float32)
                    if row < halo:
                        up_s[row] = entry_next.astype(jnp.bfloat16)
                    if row >= rows - halo:
                        down_s[row - (rows - halo)] = entry_next.astype(jnp.bfloat16)
                elif (row + 1) % part == 0:
                    store(row // part)

    if not has_next:
        @pl.when(flags[0] != number)
        def _():
            for i, kept in enumerate(saved):
                @pl.when(flags[0] == i)
                def _(kept=kept):
                    copy = pltpu.make_async_copy(kept, own_v, sems.at[len(stores)])
                    copy.start()
                    copy.wait()

            for i in range(len(stores)):
                store(i)

        wait_all(stores)


def section(number, bounds, halo, flags, offsets, kappa, forcing, arrived, following, weights, saved, result):
    rows, total, cells = forcing.shape
    fields = bounds[1] - bounds[0]
    count, per_row, block, _ = weights.shape
    has_next = bool(following)
    order = ORDERS[min(number, 1)][bounds[0] > 0]
    arrived = [arrived[i] for i in order]
    operands = [flags, offsets, kappa, in_vmem(forcing)] + arrived
    operands += following
    specs = [SMEM] * 2 + [VMEM] * (len(operands) - 2)
    operands.append(in_vmem(weights))
    specs.append(VMEM)
    extent = rows + 2 * halo
    packed = packed_rows(halo, *bounds)
    scratch = [
        pltpu.VMEM((extent, fields, cells), jnp.float32),
        pltpu.VMEM(((extent - 2 * EDGE) * cells // block, fields, block), jnp.bfloat16),
    ]
    aliases = {}
    if has_next:
        outs = [jax.ShapeDtypeStruct((n, fields, cells), jnp.bfloat16) for n in (rows, halo + packed, halo + packed)]
        out_specs = [VMEM] * 3
        if packed:
            scratch.append(pltpu.VMEM((packed * fields, cells), jnp.float32))
    else:
        outs = [jax.ShapeDtypeStruct((total, rows, cells), jnp.bfloat16)]
        out_specs = [HBM]
        scratch += [
            pltpu.VMEM((rows, fields, cells), jnp.bfloat16),
            pltpu.VMEM((fields, rows, cells), jnp.bfloat16),
            pltpu.SemaphoreType.DMA((3,)),
        ]
        operands += [in_hbm(value) for value in saved]
        specs += [HBM] * len(saved)
        if result is not None:
            aliases = {len(operands): 0}
            operands.append(result)
            specs.append(HBM)
    if packed:
        outs.append(jax.ShapeDtypeStruct((extent, cells), jnp.float32))
        out_specs.append(VMEM)
    return pl.pallas_call(
        functools.partial(section_kernel, order, number, bounds, halo, len(saved), has_next),
        in_specs=specs,
        out_shape=outs,
        out_specs=out_specs,
        input_output_aliases=aliases,
        scratch_shapes=scratch,
        compiler_params=pltpu.CompilerParams(vmem_limit_bytes=LIMIT),
        cost_estimate=pl.CostEstimate(
            flops=WEIGHT * 2 * count * per_row * block * block * fields, bytes_accessed=weights.size * 2, transcendentals=0
        ),
    )(*operands)


def local(forcing, kappa, col_blocks, remap_weights):
    n_tile = lax.axis_size("tile")
    n_section = lax.axis_size("comp")
    tile_pos = lax.axis_index("tile")
    section_pos = lax.axis_index("comp")
    weights = remap_weights[0]
    count, block = weights.shape[0], weights.shape[-1]
    rows, cells = forcing.shape[-2:]
    half = count // 2
    halo = half * block // cells + EDGE
    flags = jnp.stack([section_pos, tile_pos, jnp.full_like(tile_pos, n_tile)]).astype(jnp.int32)

    def place(s, t):
        return s * n_tile + t % n_tile

    def send(value, source, target, shift):
        pairs = [(place(source, t), place(target, t + shift)) for t in range(n_tile)]
        others = [s for s in range(n_section) if s not in (source, target)]
        if source == target:
            rest = list(zip(others[1:] + others[:1], others))
        elif source ^ 1 == target and n_section % 2 == 0:
            rest = [(target, source)] + [(s, s ^ 1) for s in others]
        else:
            rest = []
        pairs += [(place(s, t), place(to, t)) for s, to in rest for t in range(n_tile)]
        return lax.ppermute(value, AXES, pairs)

    fields = forcing.reshape(-1, rows, cells)
    marks = [fields.shape[0] * sum(SHARES[:c]) // sum(SHARES) for c in range(len(SHARES) + 1)]
    offsets, by_row, narrow, *edges = prepare(flags, col_blocks[0].T, fields, kappa[0], halo, marks)
    weights, *edges[2:] = load(flags, weights, edges[2:])
    arrivals = []
    for c in range(len(SHARES)):
        sends = [(edges[2 * c + 1], 1), (edges[2 * c], -1)][::1 - c % 2 * 2]
        arrivals.append([send(edge, 0, 0, shift) for edge, shift in sends][::1 - c % 2 * 2])
    narrow = lax.ppermute(narrow, "comp", [(s, s ^ 1) for s in range(n_section) if s ^ 1 < n_section])
    following = [[[narrow]] * len(SHARES)] + [[pair[::-1] for pair in arrivals]] * (n_section - 2) + [[[]] * len(SHARES)]
    owns = [[] for _ in SHARES]
    result = None
    for s in range(n_section):
        last = s + 1 == n_section
        leaving = []
        rates = kappa[0]
        for c, bounds in enumerate(zip(marks[:-1], marks[1:])):
            parts = list(section(
                s, bounds, halo, flags, offsets, rates, by_row, arrivals[c], following[s][c],
                weights, owns[c] if last else [], result,
            ))
            if c == 0:
                rates = parts.pop()
            if last:
                result = parts[0]
                continue
            own, up, down = parts
            owns[c].append(own)
            leaving.append([send(part, s, s + 1, shift) for part, shift in ((own, 0), (down, 1), (up, -1))])
        arrivals = leaving
    return result.reshape(forcing.shape)


def solution(mesh):
    placed = (
        P("comp", None, None, "tile", None),
        P("comp", "tile", None),
        P("comp", "tile", None),
        P("comp", "tile", None, None, None),
    )
    return jax.shard_map(
        local,
        mesh=mesh,
        in_specs=placed,
        out_specs=P("comp", None, None, "tile", None),
        check_vma=False,
    )
```

```python
import functools

import jax
import jax.numpy as jnp
from jax import lax
from jax.experimental import pallas as pl
from jax.experimental.pallas import tpu as pltpu
from jax.sharding import PartitionSpec as P

AXES = ("comp", "tile")
SHARES = (1, 1)
EDGE = 2
LIMIT = 24 << 20
ORDERS = (((-2, -1), (-1, -2)), ((-1, -2, 0), (-1, -2, 0)))
WEIGHT = 20
HBM = pl.BlockSpec(memory_space=pltpu.HBM)
VMEM = pl.BlockSpec(memory_space=pltpu.VMEM)
SMEM = pl.BlockSpec(memory_space=pltpu.SMEM)
ANY = pl.BlockSpec(memory_space=pl.ANY)


def start_all(copies):
    for copy in copies:
        copy.start()


def wait_all(copies):
    for copy in copies:
        copy.wait()


def in_hbm(value):
    return pltpu.with_memory_space_constraint(value, pltpu.HBM)


def in_vmem(value):
    return pltpu.with_memory_space_constraint(value, pltpu.VMEM)


def split(value):
    parts = []
    for _ in range(3):
        head = value.astype(jnp.bfloat16).astype(jnp.float32)
        parts.append(head)
        value = value - head
    return parts


def packed_rows(halo, start, stop):
    return 0 if start else -(-3 * halo // (stop - start))


def joined(parts, room):
    at = 0
    for part in parts:
        room[at:at + part.shape[0], :] = part
        at += part.shape[0]
    room[at:, :] = jnp.zeros((room.shape[0] - at, room.shape[1]), jnp.float32)
    return room[...].astype(jnp.bfloat16)


def prepare_kernel(halo, marks, _, forcing, kappa, *refs):
    by_row, narrow, *edges, f_v, k_v, pack, sems, k_sem = refs
    total, rows, cells = f_v.shape
    step = rows // sems.shape[0]
    loads = []
    for i in range(sems.shape[0]):
        part = pl.ds(i * step, step)
        loads.append(pltpu.make_async_copy(forcing.at[:, part], f_v.at[:, part], sems.at[i]))
    fetch = pltpu.make_async_copy(kappa, k_v, k_sem)
    fetch.start()
    start_all(loads)
    fetch.wait()
    parts = split(k_v[...])
    narrow[rows] = joined(parts, pack)
    for e, start in enumerate((0, rows - halo)):
        row = joined([part[start:start + halo] for part in parts], pack)
        tail = (edges[e].shape[0] - halo, *edges[e].shape[1:])
        edges[e][halo:] = row[:tail[0] * tail[1]].reshape(tail)
    for i, load in enumerate(loads):
        load.wait()
        turned = jnp.swapaxes(f_v[:, i * step:(i + 1) * step, :], 0, 1)
        by_row[i * step:(i + 1) * step] = turned
        for r in range(step):
            y = i * step + r
            value = turned[r].astype(jnp.bfloat16)
            narrow[y] = value
            for edge_first, edge_last, start, stop in zip(edges[0::2], edges[1::2], marks[:-1], marks[1:]):
                if y < halo:
                    edge_first[y] = value[start:stop]
                if y >= rows - halo:
                    edge_last[y - (rows - halo)] = value[start:stop]


def prepare(flags, fields, kappa, halo, marks):
    edges = [
        jax.ShapeDtypeStruct((halo + packed_rows(halo, 0, stop - start), stop - start, kappa.shape[1]), jnp.bfloat16)
        for start, stop in zip(marks[:-1], marks[1:]) for _ in range(2)
    ]
    total, rows, cells = fields.shape
    return pl.pallas_call(
        functools.partial(prepare_kernel, halo, marks),
        in_specs=[ANY, HBM, HBM],
        out_shape=[
            pltpu.VMEM((rows, total, cells), jnp.float32),
            jax.ShapeDtypeStruct((rows + 1, total, cells), jnp.bfloat16),
        ] + edges,
        out_specs=[VMEM] * (2 + len(edges)),
        scratch_shapes=[
            pltpu.VMEM((total, rows, cells), jnp.float32),
            pltpu.VMEM(kappa.shape, kappa.dtype),
            pltpu.VMEM((total, cells), jnp.float32),
            pltpu.SemaphoreType.DMA((rows // 8,)),
            pltpu.SemaphoreType.DMA,
        ],
        compiler_params=pltpu.CompilerParams(vmem_limit_bytes=LIMIT),
        cost_estimate=pl.CostEstimate(flops=0, bytes_accessed=fields.size * 12, transcendentals=0),
    )(flags, in_hbm(fields), in_hbm(kappa))


def load_kernel(n_passed, flags, columns, weights, *refs):
    held, offsets = refs[n_passed:n_passed + 2]
    c_v, sems, c_sem = refs[-3:]
    count, per_row = weights.shape[:2]
    take = pltpu.make_async_copy(columns, c_v, c_sem)
    take.start()
    loads = [pltpu.make_async_copy(weights.at[j], held.at[j], sems.at[j]) for j in range(count)]
    start_all(loads)
    take.wait()
    ahead = c_v[...] - (flags[1] * count + lax.broadcasted_iota(jnp.int32, c_v.shape, 1)) + count // 2
    every = flags[2] * count
    ahead = jnp.where(ahead < 0, ahead + every, jnp.where(ahead >= every, ahead - every, ahead))
    offsets[...] = ahead - count // 2
    wait_all(loads)

    @pl.when(flags[0] != 0)
    def _():
        def turn(i, _):
            j, k = i // per_row, i % per_row
            held[j, k] = held[j, k].T
            return 0

        lax.fori_loop(0, count * per_row, turn, 0, unroll=4)


def load(flags, columns, weights, passed):
    return pl.pallas_call(
        functools.partial(load_kernel, len(passed)),
        in_specs=[SMEM, HBM, HBM] + [ANY] * len(passed),
        out_shape=[
            pltpu.VMEM(weights.shape, weights.dtype), jax.ShapeDtypeStruct(columns.shape, columns.dtype)
        ] + [jax.ShapeDtypeStruct(p.shape, p.dtype) for p in passed],
        out_specs=[VMEM, VMEM] + [ANY] * len(passed),
        input_output_aliases={3 + i: 2 + i for i in range(len(passed))},
        scratch_shapes=[
            pltpu.VMEM(columns.shape, columns.dtype),
            pltpu.SemaphoreType.DMA((weights.shape[0],)),
            pltpu.SemaphoreType.DMA,
        ],
        compiler_params=pltpu.CompilerParams(vmem_limit_bytes=LIMIT),
        cost_estimate=pl.CostEstimate(flops=0, bytes_accessed=weights.size * 4, transcendentals=0),
    )(flags, in_hbm(columns), in_hbm(weights), *passed)


def beside_matrix(cells):
    source = lax.broadcasted_iota(jnp.int32, (2 * cells, 2 * cells), 0)
    target = lax.broadcasted_iota(jnp.int32, (2 * cells, 2 * cells), 1)
    apart = (source - target + 2 * cells) % cells
    same = (source < cells) == (target < cells)
    return jnp.where(same & ((apart == 1) | (apart == cells - 1)), 1.0, 0.0).astype(jnp.bfloat16)


def section_kernel(order, number, bounds, halo, n_saved, has_next, flags, offsets, kappa, forcing, *refs):
    refs = list(refs)
    arrived = dict(zip(order, (refs.pop(0) for _ in order)))
    upper, lower, incoming = arrived[-2], arrived[-1], arrived.get(0)
    start_chunk = bounds[0] == 0
    ahead = [refs.pop(0) for _ in range(2 if number else 1)] if has_next else []
    weights = refs.pop(0)
    saved = [refs.pop(0) for _ in range(n_saved)]
    if has_next:
        own_out, up_out, down_out = refs.pop(0), refs.pop(0), refs.pop(0)
    else:
        if bounds[0]:
            refs.pop(0)
        result = refs.pop(0)
    if has_next:
        own_v, up_s, down_s = own_out, up_out, down_out
    k_v = refs.pop(0) if start_chunk else kappa
    once, smooth, *rest = refs
    if not has_next:
        own_v, turned, sems = rest
    rows, _, cells = forcing.shape
    fields = bounds[1] - bounds[0]
    count, per_row = weights.shape[:2]
    block = weights.shape[-1]
    extent = rows + 2 * halo
    lo, hi = halo, halo + rows

    if not has_next:
        part = rows // 2
        stores = [
            pltpu.make_async_copy(
                turned.at[:, pl.ds(i * part, part)], result.at[pl.ds(bounds[0], fields), pl.ds(i * part, part)], sems.at[i]
            )
            for i in range(2)
        ]

        def store(i):
            turned[:, i * part:(i + 1) * part, :] = jnp.swapaxes(own_v[i * part:(i + 1) * part], 0, 1)
            stores[i].start()

    @pl.when(flags[0] == number)
    def _():
        mine = slice(*bounds)
        beside = beside_matrix(cells)
        top = jnp.where(flags[1] == 0, 0.0, 1.0)
        bottom = jnp.where(flags[1] == flags[2] - 1, 0.0, 1.0)
        if start_chunk:
            for edge, start in ((upper, 0), (lower, hi)):
                parts = edge[halo:].astype(jnp.float32).reshape(-1, cells)
                k_v[start:start + halo, :] = parts[:halo] + parts[halo:2 * halo] + parts[2 * halo:3 * halo]
            k_v[lo:hi, :] = kappa[...]

        def entry(i):
            if i < lo:
                return upper[i].astype(jnp.float32)
            if i >= hi:
                return lower[i - hi].astype(jnp.float32)
            value = forcing[i - lo, mine]
            if number:
                value = value + incoming[i - lo].astype(jnp.float32)
            return value

        def step(i, here, north, south, east_west):
            if i == lo:
                north = north * top
            if i == lo - 1:
                south = south * top
            if i == hi:
                north = north * bottom
            if i == hi - 1:
                south = south * bottom
            rate = k_v[i:i + 1, :]
            return (1.0 - 4.0 * rate) * here + rate * ((north + south) + east_west)

        def pair_beside(a, b):
            both = jnp.concatenate([a.astype(jnp.bfloat16), b.astype(jnp.bfloat16)], axis=1)
            total = jnp.dot(both, beside, preferred_element_type=jnp.float32)
            return total[:, :cells], total[:, cells:]

        there, after = None, entry(0)
        for i in range(0, extent, 2):
            before, here, there = there, after, entry(i + 1)
            after = entry(i + 2) if i + 2 < extent else None
            ew_here, ew_there = pair_beside(here, there)
            if i > 0:
                once[i] = step(i, here, before, there, ew_here)
            if i + 2 < extent:
                once[i + 1] = step(i + 1, there, here, after, ew_there)
        for i in range(2, extent - 2, 2):
            here, there = once[i], once[i + 1]
            ew_here, ew_there = pair_beside(here, there)
            out = i // 2 - 1
            smooth[out, :, :cells] = step(i, here, once[i - 1], there, ew_here).astype(jnp.bfloat16)
            smooth[out, :, cells:] = step(i + 1, there, here, once[i + 2], ew_there).astype(jnp.bfloat16)

        half = (halo - EDGE) * cells // block
        block_rows = block // cells
        if has_next and start_chunk:
            pack, = rest
            if number:
                up_s[halo:] = ahead[0][halo:]
                down_s[halo:] = ahead[1][halo:]
            else:
                parts = ahead[0][rows].astype(jnp.float32)
                parts = [parts[p * rows:(p + 1) * rows] for p in range(3)]
                tail = (up_s.shape[0] - halo, fields, cells)
                up_s[halo:] = joined([part[:halo] for part in parts], pack).reshape(tail)
                down_s[halo:] = joined([part[rows - halo:] for part in parts], pack).reshape(tail)
        for j in range(count):
            total = None
            for k in range(per_row):
                source = smooth[offsets[k, j] + (j + half)]
                term = lax.dot_general(
                    source, weights[j, k], (((1,), (0 if number else 1,)), ((), ())),
                    preferred_element_type=jnp.float32,
                )
                total = term if total is None else total + term
            for r in range(block_rows):
                row = j * block_rows + r
                value = total[:, r * cells:(r + 1) * cells].astype(jnp.bfloat16)
                own_v[row] = value
                if has_next:
                    if number:
                        ahead_row = ahead[0][row] if row < halo else ahead[1][row - (rows - halo)]
                    else:
                        ahead_row = ahead[0][row, mine]
                    entry_next = value.astype(jnp.float32) + ahead_row.astype(jnp.float32)
                    if row < halo:
                        up_s[row] = entry_next.astype(jnp.bfloat16)
                    if row >= rows - halo:
                        down_s[row - (rows - halo)] = entry_next.astype(jnp.bfloat16)
                elif (row + 1) % part == 0:
                    store(row // part)

    if not has_next:
        @pl.when(flags[0] != number)
        def _():
            for i, kept in enumerate(saved):
                @pl.when(flags[0] == i)
                def _(kept=kept):
                    copy = pltpu.make_async_copy(kept, own_v, sems.at[len(stores)])
                    copy.start()
                    copy.wait()

            for i in range(len(stores)):
                store(i)

        wait_all(stores)


def section(number, bounds, halo, flags, offsets, kappa, forcing, arrived, following, weights, saved, result):
    rows, total, cells = forcing.shape
    fields = bounds[1] - bounds[0]
    count, per_row, block, _ = weights.shape
    has_next = bool(following)
    order = ORDERS[min(number, 1)][bounds[0] > 0]
    arrived = [arrived[i] for i in order]
    operands = [flags, offsets, kappa, in_vmem(forcing)] + arrived
    operands += following
    specs = [SMEM] * 2 + [VMEM] * (len(operands) - 2)
    operands.append(in_vmem(weights))
    specs.append(VMEM)
    extent = rows + 2 * halo
    packed = packed_rows(halo, *bounds)
    scratch = [
        pltpu.VMEM((extent, fields, cells), jnp.float32),
        pltpu.VMEM(((extent - 2 * EDGE) * cells // block, fields, block), jnp.bfloat16),
    ]
    aliases = {}
    if has_next:
        outs = [jax.ShapeDtypeStruct((n, fields, cells), jnp.bfloat16) for n in (rows, halo + packed, halo + packed)]
        out_specs = [VMEM] * 3
        if packed:
            scratch.append(pltpu.VMEM((packed * fields, cells), jnp.float32))
    else:
        outs = [jax.ShapeDtypeStruct((total, rows, cells), jnp.bfloat16)]
        out_specs = [HBM]
        scratch += [
            pltpu.VMEM((rows, fields, cells), jnp.bfloat16),
            pltpu.VMEM((fields, rows, cells), jnp.bfloat16),
            pltpu.SemaphoreType.DMA((3,)),
        ]
        operands += [in_hbm(value) for value in saved]
        specs += [HBM] * len(saved)
        if result is not None:
            aliases = {len(operands): 0}
            operands.append(result)
            specs.append(HBM)
    if packed:
        outs.append(jax.ShapeDtypeStruct((extent, cells), jnp.float32))
        out_specs.append(VMEM)
    return pl.pallas_call(
        functools.partial(section_kernel, order, number, bounds, halo, len(saved), has_next),
        in_specs=specs,
        out_shape=outs,
        out_specs=out_specs,
        input_output_aliases=aliases,
        scratch_shapes=scratch,
        compiler_params=pltpu.CompilerParams(vmem_limit_bytes=LIMIT),
        cost_estimate=pl.CostEstimate(
            flops=WEIGHT * 2 * count * per_row * block * block * fields, bytes_accessed=weights.size * 2, transcendentals=0
        ),
    )(*operands)


def local(forcing, kappa, col_blocks, remap_weights):
    n_tile = lax.axis_size("tile")
    n_section = lax.axis_size("comp")
    tile_pos = lax.axis_index("tile")
    section_pos = lax.axis_index("comp")
    weights = remap_weights[0]
    count, block = weights.shape[0], weights.shape[-1]
    rows, cells = forcing.shape[-2:]
    half = count // 2
    halo = half * block // cells + EDGE
    flags = jnp.stack([section_pos, tile_pos, jnp.full_like(tile_pos, n_tile)]).astype(jnp.int32)

    def place(s, t):
        return s * n_tile + t % n_tile

    def send(value, source, target, shift):
        pairs = [(place(source, t), place(target, t + shift)) for t in range(n_tile)]
        others = [s for s in range(n_section) if s not in (source, target)]
        if source == target:
            rest = list(zip(others[1:] + others[:1], others))
        elif n_section % 2 == 0 and source % 2:
            rest = [(target, target ^ 1), (target ^ 1, source ^ 1), (source ^ 1, source)]
            rest += [(s, s ^ 1) for s in others if s not in (target ^ 1, source ^ 1)]
        elif source ^ 1 == target and n_section % 2 == 0:
            rest = [(target, source)] + [(s, s ^ 1) for s in others]
        else:
            rest = []
        pairs += [(place(s, t), place(to, t)) for s, to in rest for t in range(n_tile)]
        return lax.ppermute(value, AXES, pairs)

    fields = forcing.reshape(-1, rows, cells)
    marks = [fields.shape[0] * sum(SHARES[:c]) // sum(SHARES) for c in range(len(SHARES) + 1)]
    by_row, narrow, *edges = prepare(flags, fields, kappa[0], halo, marks)
    weights, offsets, *edges[2:] = load(flags, col_blocks[0].T, weights, edges[2:])
    arrivals = []
    for c in range(len(SHARES)):
        sends = [(edges[2 * c + 1], 1), (edges[2 * c], -1)][::1 - c % 2 * 2]
        arrivals.append([send(edge, 0, 0, shift) for edge, shift in sends][::1 - c % 2 * 2])
    narrow = lax.ppermute(narrow, "comp", [(s, s ^ 1) for s in range(n_section) if s ^ 1 < n_section])
    following = [[[narrow]] * len(SHARES)] + [[pair[::-1] for pair in arrivals]] * (n_section - 2) + [[[]] * len(SHARES)]
    owns = [[] for _ in SHARES]
    result = None
    for s in range(n_section):
        last = s + 1 == n_section
        leaving = []
        rates = kappa[0]
        for c, bounds in enumerate(zip(marks[:-1], marks[1:])):
            parts = list(section(
                s, bounds, halo, flags, offsets, rates, by_row, arrivals[c], following[s][c],
                weights, owns[c] if last else [], result,
            ))
            if c == 0:
                rates = parts.pop()
            if last:
                result = parts[0]
                continue
            own, up, down = parts
            owns[c].append(own)
            leaving.append([send(part, s, s + 1, shift) for part, shift in ((own, 0), (down, 1), (up, -1))])
        arrivals = leaving
    return result.reshape(forcing.shape)


def solution(mesh):
    placed = (
        P("comp", None, None, "tile", None),
        P("comp", "tile", None),
        P("comp", "tile", None),
        P("comp", "tile", None, None, None),
    )
    return jax.shard_map(
        local,
        mesh=mesh,
        in_specs=placed,
        out_specs=P("comp", None, None, "tile", None),
        check_vma=False,
    )
```

```python
import functools

import jax
import jax.numpy as jnp
from jax import lax
from jax.experimental import pallas as pl
from jax.experimental.pallas import tpu as pltpu
from jax.sharding import PartitionSpec as P

AXES = ("comp", "tile")
SHARES = (1, 1)
EDGE = 2
LIMIT = 24 << 20
ORDERS = (((0, 1), (0, 1)), ((-2, -1, 0), (-1, -2, 0)))
WEIGHT = 20
HBM = pl.BlockSpec(memory_space=pltpu.HBM)
VMEM = pl.BlockSpec(memory_space=pltpu.VMEM)
SMEM = pl.BlockSpec(memory_space=pltpu.SMEM)
ANY = pl.BlockSpec(memory_space=pl.ANY)


def start_all(copies):
    for copy in copies:
        copy.start()


def wait_all(copies):
    for copy in copies:
        copy.wait()


def in_hbm(value):
    return pltpu.with_memory_space_constraint(value, pltpu.HBM)


def in_vmem(value):
    return pltpu.with_memory_space_constraint(value, pltpu.VMEM)


def split(value):
    parts = []
    for _ in range(3):
        head = value.astype(jnp.bfloat16).astype(jnp.float32)
        parts.append(head)
        value = value - head
    return parts


def packed_rows(halo, start, stop):
    return 0 if start else -(-3 * halo // (stop - start))


def joined(parts, room):
    at = 0
    for part in parts:
        room[at:at + part.shape[0], :] = part
        at += part.shape[0]
    room[at:, :] = jnp.zeros((room.shape[0] - at, room.shape[1]), jnp.float32)
    return room[...].astype(jnp.bfloat16)


def prepare_kernel(halo, marks, _, forcing, kappa, *refs):
    by_row, narrow, *edges, f_v, k_v, pack, sems, k_sem = refs
    total, rows, cells = f_v.shape
    step = rows // sems.shape[0]
    loads = []
    for i in range(sems.shape[0]):
        part = pl.ds(i * step, step)
        loads.append(pltpu.make_async_copy(forcing.at[:, part], f_v.at[:, part], sems.at[i]))
    fetch = pltpu.make_async_copy(kappa, k_v, k_sem)
    fetch.start()
    start_all(loads)
    fetch.wait()
    odd = lax.rem(lax.axis_index("tile"), 2) == 1
    swapped = odd & (lax.axis_index("comp") == 0)

    def write(edges):
        parts = split(k_v[...])
        narrow[rows] = joined(parts, pack)
        for e, start in enumerate((0, rows - halo)):
            row = joined([part[start:start + halo] for part in parts], pack)
            tail = (edges[e].shape[0] - halo, *edges[e].shape[1:])
            edges[e][halo:] = row[:tail[0] * tail[1]].reshape(tail)
        for i, load in enumerate(loads):
            load.wait()
            turned = jnp.swapaxes(f_v[:, i * step:(i + 1) * step, :], 0, 1)
            by_row[i * step:(i + 1) * step] = turned
            for r in range(step):
                y = i * step + r
                value = turned[r].astype(jnp.bfloat16)
                narrow[y] = value
                for edge_first, edge_last, start, stop in zip(edges[0::2], edges[1::2], marks[:-1], marks[1:]):
                    if y < halo:
                        edge_first[y] = value[start:stop]
                    if y >= rows - halo:
                        edge_last[y - (rows - halo)] = value[start:stop]

    @pl.when(swapped)
    def _():
        write([edge for pair in zip(edges[1::2], edges[0::2]) for edge in pair])

    @pl.when(jnp.logical_not(swapped))
    def _():
        write(edges)


def prepare(flags, fields, kappa, halo, marks):
    edges = [
        jax.ShapeDtypeStruct((halo + packed_rows(halo, 0, stop - start), stop - start, kappa.shape[1]), jnp.bfloat16)
        for start, stop in zip(marks[:-1], marks[1:]) for _ in range(2)
    ]
    total, rows, cells = fields.shape
    return pl.pallas_call(
        functools.partial(prepare_kernel, halo, marks),
        in_specs=[ANY, HBM, HBM],
        out_shape=[
            pltpu.VMEM((rows, total, cells), jnp.float32),
            jax.ShapeDtypeStruct((rows + 1, total, cells), jnp.bfloat16),
        ] + edges,
        out_specs=[VMEM] * (2 + len(edges)),
        scratch_shapes=[
            pltpu.VMEM((total, rows, cells), jnp.float32),
            pltpu.VMEM(kappa.shape, kappa.dtype),
            pltpu.VMEM((total, cells), jnp.float32),
            pltpu.SemaphoreType.DMA((rows // 8,)),
            pltpu.SemaphoreType.DMA,
        ],
        compiler_params=pltpu.CompilerParams(vmem_limit_bytes=LIMIT),
        cost_estimate=pl.CostEstimate(flops=0, bytes_accessed=fields.size * 12, transcendentals=0),
    )(flags, in_hbm(fields), in_hbm(kappa))


def load_kernel(n_passed, flags, columns, weights, *refs):
    held, offsets = refs[n_passed:n_passed + 2]
    c_v, sems, c_sem = refs[-3:]
    count, per_row = weights.shape[:2]
    take = pltpu.make_async_copy(columns, c_v, c_sem)
    take.start()
    loads = [pltpu.make_async_copy(weights.at[j], held.at[j], sems.at[j]) for j in range(count)]
    start_all(loads)
    take.wait()
    ahead = c_v[...] - (flags[1] * count + lax.broadcasted_iota(jnp.int32, c_v.shape, 1)) + count // 2
    every = flags[2] * count
    ahead = jnp.where(ahead < 0, ahead + every, jnp.where(ahead >= every, ahead - every, ahead))
    offsets[...] = ahead - count // 2
    wait_all(loads)

    @pl.when(flags[0] != 0)
    def _():
        def turn(i, _):
            j, k = i // per_row, i % per_row
            held[j, k] = held[j, k].T
            return 0

        lax.fori_loop(0, count * per_row, turn, 0, unroll=4)


def load(flags, columns, weights, passed):
    return pl.pallas_call(
        functools.partial(load_kernel, len(passed)),
        in_specs=[SMEM, HBM, HBM] + [ANY] * len(passed),
        out_shape=[
            pltpu.VMEM(weights.shape, weights.dtype), jax.ShapeDtypeStruct(columns.shape, columns.dtype)
        ] + [jax.ShapeDtypeStruct(p.shape, p.dtype) for p in passed],
        out_specs=[VMEM, VMEM] + [ANY] * len(passed),
        input_output_aliases={3 + i: 2 + i for i in range(len(passed))},
        scratch_shapes=[
            pltpu.VMEM(columns.shape, columns.dtype),
            pltpu.SemaphoreType.DMA((weights.shape[0],)),
            pltpu.SemaphoreType.DMA,
        ],
        compiler_params=pltpu.CompilerParams(vmem_limit_bytes=LIMIT),
        cost_estimate=pl.CostEstimate(flops=0, bytes_accessed=weights.size * 4, transcendentals=0),
    )(flags, in_hbm(columns), in_hbm(weights), *passed)


def beside_matrix(cells):
    source = lax.broadcasted_iota(jnp.int32, (2 * cells, 2 * cells), 0)
    target = lax.broadcasted_iota(jnp.int32, (2 * cells, 2 * cells), 1)
    apart = (source - target + 2 * cells) % cells
    same = (source < cells) == (target < cells)
    return jnp.where(same & ((apart == 1) | (apart == cells - 1)), 1.0, 0.0).astype(jnp.bfloat16)


def section_kernel(order, number, bounds, halo, n_saved, has_next, flags, offsets, kappa, forcing, *refs):
    refs = list(refs)
    arrived = [refs.pop(0) for _ in order]
    start_chunk = bounds[0] == 0
    ahead = [refs.pop(0) for _ in range(2 if number else 1)] if has_next else []
    weights = refs.pop(0)
    saved = [refs.pop(0) for _ in range(n_saved)]
    if has_next:
        own_out, up_out, down_out = refs.pop(0), refs.pop(0), refs.pop(0)
    else:
        if bounds[0]:
            refs.pop(0)
        result = refs.pop(0)
    if has_next:
        own_v, up_s, down_s = own_out, up_out, down_out
    k_v = refs.pop(0) if start_chunk else kappa
    once, smooth, *rest = refs
    if not has_next:
        own_v, turned, sems = rest
    rows, _, cells = forcing.shape
    fields = bounds[1] - bounds[0]
    count, per_row = weights.shape[:2]
    block = weights.shape[-1]
    extent = rows + 2 * halo
    lo, hi = halo, halo + rows

    if not has_next:
        part = rows // 2
        stores = [
            pltpu.make_async_copy(
                turned.at[:, pl.ds(i * part, part)], result.at[pl.ds(bounds[0], fields), pl.ds(i * part, part)], sems.at[i]
            )
            for i in range(2)
        ]

        def store(i):
            turned[:, i * part:(i + 1) * part, :] = jnp.swapaxes(own_v[i * part:(i + 1) * part], 0, 1)
            stores[i].start()

    def active(upper, lower, incoming=None):
        mine = slice(*bounds)
        beside = beside_matrix(cells)
        top = jnp.where(flags[1] == 0, 0.0, 1.0)
        bottom = jnp.where(flags[1] == flags[2] - 1, 0.0, 1.0)
        if start_chunk:
            for edge, start in ((upper, 0), (lower, hi)):
                parts = edge[halo:].astype(jnp.float32).reshape(-1, cells)
                k_v[start:start + halo, :] = parts[:halo] + parts[halo:2 * halo] + parts[2 * halo:3 * halo]
            k_v[lo:hi, :] = kappa[...]

        def entry(i):
            if i < lo:
                return upper[i].astype(jnp.float32)
            if i >= hi:
                return lower[i - hi].astype(jnp.float32)
            value = forcing[i - lo, mine]
            if number:
                value = value + incoming[i - lo].astype(jnp.float32)
            return value

        def step(i, here, north, south, east_west):
            if i == lo:
                north = north * top
            if i == lo - 1:
                south = south * top
            if i == hi:
                north = north * bottom
            if i == hi - 1:
                south = south * bottom
            rate = k_v[i:i + 1, :]
            return (1.0 - 4.0 * rate) * here + rate * ((north + south) + east_west)

        def pair_beside(a, b):
            both = jnp.concatenate([a.astype(jnp.bfloat16), b.astype(jnp.bfloat16)], axis=1)
            total = jnp.dot(both, beside, preferred_element_type=jnp.float32)
            return total[:, :cells], total[:, cells:]

        there, after = None, entry(0)
        for i in range(0, extent, 2):
            before, here, there = there, after, entry(i + 1)
            after = entry(i + 2) if i + 2 < extent else None
            ew_here, ew_there = pair_beside(here, there)
            if i > 0:
                once[i] = step(i, here, before, there, ew_here)
            if i + 2 < extent:
                once[i + 1] = step(i + 1, there, here, after, ew_there)
        for i in range(2, extent - 2, 2):
            here, there = once[i], once[i + 1]
            ew_here, ew_there = pair_beside(here, there)
            out = i // 2 - 1
            smooth[out, :, :cells] = step(i, here, once[i - 1], there, ew_here).astype(jnp.bfloat16)
            smooth[out, :, cells:] = step(i + 1, there, here, once[i + 2], ew_there).astype(jnp.bfloat16)

        half = (halo - EDGE) * cells // block
        block_rows = block // cells
        if has_next and start_chunk:
            pack, = rest
            if number:
                up_s[halo:] = ahead[0][halo:]
                down_s[halo:] = ahead[1][halo:]
            else:
                parts = ahead[0][rows].astype(jnp.float32)
                parts = [parts[p * rows:(p + 1) * rows] for p in range(3)]
                tail = (up_s.shape[0] - halo, fields, cells)
                up_s[halo:] = joined([part[:halo] for part in parts], pack).reshape(tail)
                down_s[halo:] = joined([part[rows - halo:] for part in parts], pack).reshape(tail)
        for j in range(count):
            total = None
            for k in range(per_row):
                source = smooth[offsets[k, j] + (j + half)]
                term = lax.dot_general(
                    source, weights[j, k], (((1,), (0 if number else 1,)), ((), ())),
                    preferred_element_type=jnp.float32,
                )
                total = term if total is None else total + term
            for r in range(block_rows):
                row = j * block_rows + r
                value = total[:, r * cells:(r + 1) * cells].astype(jnp.bfloat16)
                own_v[row] = value
                if has_next:
                    if number:
                        ahead_row = ahead[0][row] if row < halo else ahead[1][row - (rows - halo)]
                    else:
                        ahead_row = ahead[0][row, mine]
                    entry_next = value.astype(jnp.float32) + ahead_row.astype(jnp.float32)
                    if row < halo:
                        up_s[row] = entry_next.astype(jnp.bfloat16)
                    if row >= rows - halo:
                        down_s[row - (rows - halo)] = entry_next.astype(jnp.bfloat16)
                elif (row + 1) % part == 0:
                    store(row // part)

    if number:
        @pl.when(flags[0] == number)
        def _():
            by_name = dict(zip(order, arrived))
            active(by_name[-2], by_name[-1], by_name[0])
    else:
        for odd in range(2):
            @pl.when((flags[0] == number) & (lax.rem(flags[1], 2) == odd))
            def _(odd=odd):
                active(arrived[1 - odd], arrived[odd])

    if not has_next:
        @pl.when(flags[0] != number)
        def _():
            for i, kept in enumerate(saved):
                @pl.when(flags[0] == i)
                def _(kept=kept):
                    copy = pltpu.make_async_copy(kept, own_v, sems.at[len(stores)])
                    copy.start()
                    copy.wait()

            for i in range(len(stores)):
                store(i)

        wait_all(stores)


def section(number, bounds, halo, flags, offsets, kappa, forcing, arrived, following, weights, saved, result):
    rows, total, cells = forcing.shape
    fields = bounds[1] - bounds[0]
    count, per_row, block, _ = weights.shape
    has_next = bool(following)
    order = ORDERS[min(number, 1)][bounds[0] > 0]
    arrived = [arrived[i] for i in order]
    operands = [flags, offsets, kappa, in_vmem(forcing)] + arrived
    operands += following
    specs = [SMEM] * 2 + [VMEM] * (len(operands) - 2)
    operands.append(in_vmem(weights))
    specs.append(VMEM)
    extent = rows + 2 * halo
    packed = packed_rows(halo, *bounds)
    scratch = [
        pltpu.VMEM((extent, fields, cells), jnp.float32),
        pltpu.VMEM(((extent - 2 * EDGE) * cells // block, fields, block), jnp.bfloat16),
    ]
    aliases = {}
    if has_next:
        outs = [jax.ShapeDtypeStruct((n, fields, cells), jnp.bfloat16) for n in (rows, halo + packed, halo + packed)]
        out_specs = [VMEM] * 3
        if packed:
            scratch.append(pltpu.VMEM((packed * fields, cells), jnp.float32))
    else:
        outs = [jax.ShapeDtypeStruct((total, rows, cells), jnp.bfloat16)]
        out_specs = [HBM]
        scratch += [
            pltpu.VMEM((rows, fields, cells), jnp.bfloat16),
            pltpu.VMEM((fields, rows, cells), jnp.bfloat16),
            pltpu.SemaphoreType.DMA((3,)),
        ]
        operands += [in_hbm(value) for value in saved]
        specs += [HBM] * len(saved)
        if result is not None:
            aliases = {len(operands): 0}
            operands.append(result)
            specs.append(HBM)
    if packed:
        outs.append(jax.ShapeDtypeStruct((extent, cells), jnp.float32))
        out_specs.append(VMEM)
    return pl.pallas_call(
        functools.partial(section_kernel, order, number, bounds, halo, len(saved), has_next),
        in_specs=specs,
        out_shape=outs,
        out_specs=out_specs,
        input_output_aliases=aliases,
        scratch_shapes=scratch,
        compiler_params=pltpu.CompilerParams(vmem_limit_bytes=LIMIT),
        cost_estimate=pl.CostEstimate(
            flops=WEIGHT * 2 * count * per_row * block * block * fields, bytes_accessed=weights.size * 2, transcendentals=0
        ),
    )(*operands)


def local(forcing, kappa, col_blocks, remap_weights):
    n_tile = lax.axis_size("tile")
    n_section = lax.axis_size("comp")
    tile_pos = lax.axis_index("tile")
    section_pos = lax.axis_index("comp")
    weights = remap_weights[0]
    count, block = weights.shape[0], weights.shape[-1]
    rows, cells = forcing.shape[-2:]
    half = count // 2
    halo = half * block // cells + EDGE
    flags = jnp.stack([section_pos, tile_pos, jnp.full_like(tile_pos, n_tile)]).astype(jnp.int32)

    def place(s, t):
        return s * n_tile + t % n_tile

    def send(value, source, target, shift):
        pairs = [(place(source, t), place(target, t + shift)) for t in range(n_tile)]
        others = [s for s in range(n_section) if s not in (source, target)]
        if n_section % 2 == 0 and source % 2:
            rest = [(target, target ^ 1), (target ^ 1, source ^ 1), (source ^ 1, source)]
            rest += [(s, s ^ 1) for s in others if s not in (target ^ 1, source ^ 1)]
        elif source ^ 1 == target and n_section % 2 == 0:
            rest = [(target, source)] + [(s, s ^ 1) for s in others]
        else:
            rest = []
        pairs += [(place(s, t), place(to, t)) for s, to in rest for t in range(n_tile)]
        return lax.ppermute(value, AXES, pairs)

    def exchange(value, first):
        pairs = [(place(0, t), place(0, t + 1 if t % 2 == first else t - 1)) for t in range(n_tile)]
        pairs += [(place(s, t), place((s - 2) % (n_section - 1) + 1, t)) for s in range(1, n_section) for t in range(n_tile)]
        return lax.ppermute(value, AXES, pairs)

    fields = forcing.reshape(-1, rows, cells)
    marks = [fields.shape[0] * sum(SHARES[:c]) // sum(SHARES) for c in range(len(SHARES) + 1)]
    by_row, narrow, *edges = prepare(flags, fields, kappa[0], halo, marks)
    weights, offsets, *edges[2:] = load(flags, col_blocks[0].T, weights, edges[2:])
    arrivals = []
    for c in range(len(SHARES)):
        arrivals.append([exchange(edges[2 * c + 1], 0), exchange(edges[2 * c], 1)])
    narrow = lax.ppermute(narrow, "comp", [(s, s ^ 1) for s in range(n_section) if s ^ 1 < n_section])
    following = [[[narrow]] * len(SHARES)] + [[pair[::-1] for pair in arrivals]] * (n_section - 2) + [[[]] * len(SHARES)]
    owns = [[] for _ in SHARES]
    result = None
    for s in range(n_section):
        last = s + 1 == n_section
        leaving = []
        rates = kappa[0]
        for c, bounds in enumerate(zip(marks[:-1], marks[1:])):
            parts = list(section(
                s, bounds, halo, flags, offsets, rates, by_row, arrivals[c], following[s][c],
                weights, owns[c] if last else [], result,
            ))
            if c == 0:
                rates = parts.pop()
            if last:
                result = parts[0]
                continue
            own, up, down = parts
            owns[c].append(own)
            leaving.append([send(part, s, s + 1, shift) for part, shift in ((own, 0), (down, 1), (up, -1))])
        arrivals = leaving
    return result.reshape(forcing.shape)


def solution(mesh):
    placed = (
        P("comp", None, None, "tile", None),
        P("comp", "tile", None),
        P("comp", "tile", None),
        P("comp", "tile", None, None, None),
    )
    return jax.shard_map(
        local,
        mesh=mesh,
        in_specs=placed,
        out_specs=P("comp", None, None, "tile", None),
        check_vma=False,
    )
```

```python
import functools

import jax
import jax.numpy as jnp
from jax import lax
from jax.experimental import pallas as pl
from jax.experimental.pallas import tpu as pltpu
from jax.sharding import PartitionSpec as P

AXES = ("comp", "tile")
SHARES = (1, 1)
PAIRS = 4
EDGE = 2
LIMIT = 24 << 20
ORDERS = (((0, 1), (0, 1)), ((-2, -1, 0), (-1, -2, 0)))
WEIGHT = 20
HBM = pl.BlockSpec(memory_space=pltpu.HBM)
VMEM = pl.BlockSpec(memory_space=pltpu.VMEM)
SMEM = pl.BlockSpec(memory_space=pltpu.SMEM)
ANY = pl.BlockSpec(memory_space=pl.ANY)


def start_all(copies):
    for copy in copies:
        copy.start()


def wait_all(copies):
    for copy in copies:
        copy.wait()


def in_hbm(value):
    return pltpu.with_memory_space_constraint(value, pltpu.HBM)


def in_vmem(value):
    return pltpu.with_memory_space_constraint(value, pltpu.VMEM)


def split(value):
    parts = []
    for _ in range(3):
        head = value.astype(jnp.bfloat16).astype(jnp.float32)
        parts.append(head)
        value = value - head
    return parts


def packed_rows(halo, start, stop):
    return 0 if start else -(-3 * halo // (stop - start))


def joined(parts, room):
    at = 0
    for part in parts:
        room[at:at + part.shape[0], :] = part
        at += part.shape[0]
    room[at:, :] = jnp.zeros((room.shape[0] - at, room.shape[1]), jnp.float32)
    return room[...].astype(jnp.bfloat16)


def prepare_kernel(halo, marks, _, forcing, kappa, *refs):
    by_row, narrow, *edges, f_v, k_v, pack, sems, k_sem = refs
    total, rows, cells = f_v.shape
    step = rows // sems.shape[0]
    loads = []
    for i in range(sems.shape[0]):
        part = pl.ds(i * step, step)
        loads.append(pltpu.make_async_copy(forcing.at[:, part], f_v.at[:, part], sems.at[i]))
    fetch = pltpu.make_async_copy(kappa, k_v, k_sem)
    fetch.start()
    start_all(loads)
    fetch.wait()
    odd = lax.rem(lax.axis_index("tile"), 2) == 1
    swapped = odd & (lax.axis_index("comp") == 0)

    def write(edges):
        parts = split(k_v[...])
        narrow[rows] = joined(parts, pack)
        for e, start in enumerate((0, rows - halo)):
            row = joined([part[start:start + halo] for part in parts], pack)
            tail = (edges[e].shape[0] - halo, *edges[e].shape[1:])
            edges[e][halo:] = row[:tail[0] * tail[1]].reshape(tail)
        for i, load in enumerate(loads):
            load.wait()
            turned = jnp.swapaxes(f_v[:, i * step:(i + 1) * step, :], 0, 1)
            by_row[i * step:(i + 1) * step] = turned
            for r in range(step):
                y = i * step + r
                value = turned[r].astype(jnp.bfloat16)
                narrow[y] = value
                for edge_first, edge_last, start, stop in zip(edges[0::2], edges[1::2], marks[:-1], marks[1:]):
                    if y < halo:
                        edge_first[y] = value[start:stop]
                    if y >= rows - halo:
                        edge_last[y - (rows - halo)] = value[start:stop]

    @pl.when(swapped)
    def _():
        write([edge for pair in zip(edges[1::2], edges[0::2]) for edge in pair])

    @pl.when(jnp.logical_not(swapped))
    def _():
        write(edges)


def prepare(flags, fields, kappa, halo, marks):
    edges = [
        jax.ShapeDtypeStruct((halo + packed_rows(halo, 0, stop - start), stop - start, kappa.shape[1]), jnp.bfloat16)
        for start, stop in zip(marks[:-1], marks[1:]) for _ in range(2)
    ]
    total, rows, cells = fields.shape
    return pl.pallas_call(
        functools.partial(prepare_kernel, halo, marks),
        in_specs=[ANY, HBM, HBM],
        out_shape=[
            pltpu.VMEM((rows, total, cells), jnp.float32),
            jax.ShapeDtypeStruct((rows + 1, total, cells), jnp.bfloat16),
        ] + edges,
        out_specs=[VMEM] * (2 + len(edges)),
        scratch_shapes=[
            pltpu.VMEM((total, rows, cells), jnp.float32),
            pltpu.VMEM(kappa.shape, kappa.dtype),
            pltpu.VMEM((total, cells), jnp.float32),
            pltpu.SemaphoreType.DMA((rows // 8,)),
            pltpu.SemaphoreType.DMA,
        ],
        compiler_params=pltpu.CompilerParams(vmem_limit_bytes=LIMIT),
        cost_estimate=pl.CostEstimate(flops=0, bytes_accessed=fields.size * 12, transcendentals=0),
    )(flags, in_hbm(fields), in_hbm(kappa))


def load_kernel(n_passed, flags, columns, weights, *refs):
    held, offsets = refs[n_passed:n_passed + 2]
    c_v, sems, c_sem = refs[-3:]
    count, per_row = weights.shape[:2]
    take = pltpu.make_async_copy(columns, c_v, c_sem)
    take.start()
    loads = [pltpu.make_async_copy(weights.at[j], held.at[j], sems.at[j]) for j in range(count)]
    start_all(loads)
    take.wait()
    ahead = c_v[...] - (flags[1] * count + lax.broadcasted_iota(jnp.int32, c_v.shape, 1)) + count // 2
    every = flags[2] * count
    ahead = jnp.where(ahead < 0, ahead + every, jnp.where(ahead >= every, ahead - every, ahead))
    offsets[...] = ahead - count // 2
    wait_all(loads)

    @pl.when(flags[0] != 0)
    def _():
        def turn(i, _):
            j, k = i // per_row, i % per_row
            held[j, k] = held[j, k].T
            return 0

        lax.fori_loop(0, count * per_row, turn, 0, unroll=4)


def load(flags, columns, weights, passed):
    return pl.pallas_call(
        functools.partial(load_kernel, len(passed)),
        in_specs=[SMEM, HBM, HBM] + [ANY] * len(passed),
        out_shape=[
            pltpu.VMEM(weights.shape, weights.dtype), jax.ShapeDtypeStruct(columns.shape, columns.dtype)
        ] + [jax.ShapeDtypeStruct(p.shape, p.dtype) for p in passed],
        out_specs=[VMEM, VMEM] + [ANY] * len(passed),
        input_output_aliases={3 + i: 2 + i for i in range(len(passed))},
        scratch_shapes=[
            pltpu.VMEM(columns.shape, columns.dtype),
            pltpu.SemaphoreType.DMA((weights.shape[0],)),
            pltpu.SemaphoreType.DMA,
        ],
        compiler_params=pltpu.CompilerParams(vmem_limit_bytes=LIMIT),
        cost_estimate=pl.CostEstimate(flops=0, bytes_accessed=weights.size * 4, transcendentals=0),
    )(flags, in_hbm(columns), in_hbm(weights), *passed)


def beside_matrix(cells):
    source = lax.broadcasted_iota(jnp.int32, (2 * cells, 2 * cells), 0)
    target = lax.broadcasted_iota(jnp.int32, (2 * cells, 2 * cells), 1)
    apart = (source - target + 2 * cells) % cells
    same = (source < cells) == (target < cells)
    return jnp.where(same & ((apart == 1) | (apart == cells - 1)), 1.0, 0.0).astype(jnp.bfloat16)


def section_kernel(order, number, bounds, halo, n_saved, has_next, flags, offsets, kappa, forcing, *refs):
    refs = list(refs)
    arrived = [refs.pop(0) for _ in order]
    start_chunk = bounds[0] == 0
    ahead = [refs.pop(0) for _ in range(2 if number else 1)] if has_next else []
    weights = refs.pop(0)
    saved = [refs.pop(0) for _ in range(n_saved)]
    if has_next:
        own_out, up_out, down_out = refs.pop(0), refs.pop(0), refs.pop(0)
    else:
        if bounds[0]:
            refs.pop(0)
        result = refs.pop(0)
    if has_next:
        own_v, up_s, down_s = own_out, up_out, down_out
    k_v = refs.pop(0) if start_chunk else kappa
    once, smooth, *rest = refs
    if not has_next:
        own_v, turned, sems = rest
    rows, _, cells = forcing.shape
    fields = bounds[1] - bounds[0]
    count, per_row = weights.shape[:2]
    block = weights.shape[-1]
    extent = rows + 2 * halo
    lo, hi = halo, halo + rows

    if not has_next:
        part = rows // 2
        stores = [
            pltpu.make_async_copy(
                turned.at[:, pl.ds(i * part, part)], result.at[pl.ds(bounds[0], fields), pl.ds(i * part, part)], sems.at[i]
            )
            for i in range(2)
        ]

        def store(i):
            turned[:, i * part:(i + 1) * part, :] = jnp.swapaxes(own_v[i * part:(i + 1) * part], 0, 1)
            stores[i].start()

    def active(upper, lower, incoming=None):
        mine = slice(*bounds)
        beside = beside_matrix(cells)
        top = jnp.where(flags[1] == 0, 0.0, 1.0)
        bottom = jnp.where(flags[1] == flags[2] - 1, 0.0, 1.0)
        if start_chunk:
            for edge, start in ((upper, 0), (lower, hi)):
                parts = edge[halo:].astype(jnp.float32).reshape(-1, cells)
                k_v[start:start + halo, :] = parts[:halo] + parts[halo:2 * halo] + parts[2 * halo:3 * halo]
            k_v[lo:hi, :] = kappa[...]

        def entry(i):
            if i < lo:
                return upper[i].astype(jnp.float32)
            if i >= hi:
                return lower[i - hi].astype(jnp.float32)
            value = forcing[i - lo, mine]
            if number:
                value = value + incoming[i - lo].astype(jnp.float32)
            return value

        def step(i, here, north, south, east_west):
            if i == lo:
                north = north * top
            if i == lo - 1:
                south = south * top
            if i == hi:
                north = north * bottom
            if i == hi - 1:
                south = south * bottom
            rate = k_v[i:i + 1, :]
            return (1.0 - 4.0 * rate) * here + rate * ((north + south) + east_west)

        def sums_beside(values):
            pairs = [
                jnp.concatenate([a.astype(jnp.bfloat16), b.astype(jnp.bfloat16)], axis=1)
                for a, b in zip(values[0::2], values[1::2])
            ]
            total = jnp.dot(jnp.concatenate(pairs, axis=0), beside, preferred_element_type=jnp.float32)
            sums = []
            for p in range(len(pairs)):
                both = total[p * fields:(p + 1) * fields]
                sums += [both[:, :cells], both[:, cells:]]
            return sums

        def sweep(fetch, start, stop, put):
            for i in range(start, stop, 2 * PAIRS):
                group = range(i, min(i + 2 * PAIRS, stop))
                values = [fetch(r) for r in group]
                sums = sums_beside(values)
                around = [fetch(i - 1)] + values + [fetch(group[-1] + 1)]
                for g, r in enumerate(group):
                    put(r, around[g], around[g + 1], around[g + 2], sums[g])

        def put_once(r, north, here, south, east_west):
            if 0 < r < extent - 1:
                once[r] = step(r, here, north, south, east_west)

        def put_smooth(r, north, here, south, east_west):
            side = slice(0, cells) if r % 2 == 0 else slice(cells, 2 * cells)
            smooth[r // 2 - 1, :, side] = step(r, here, north, south, east_west).astype(jnp.bfloat16)

        sweep(lambda r: entry(r) if 0 <= r < extent else None, 0, extent, put_once)
        sweep(lambda r: once[r], 2, extent - 2, put_smooth)

        half = (halo - EDGE) * cells // block
        block_rows = block // cells
        if has_next and start_chunk:
            pack, = rest
            if number:
                up_s[halo:] = ahead[0][halo:]
                down_s[halo:] = ahead[1][halo:]
            else:
                parts = ahead[0][rows].astype(jnp.float32)
                parts = [parts[p * rows:(p + 1) * rows] for p in range(3)]
                tail = (up_s.shape[0] - halo, fields, cells)
                up_s[halo:] = joined([part[:halo] for part in parts], pack).reshape(tail)
                down_s[halo:] = joined([part[rows - halo:] for part in parts], pack).reshape(tail)
        for j in range(count):
            total = None
            for k in range(per_row):
                source = smooth[offsets[k, j] + (j + half)]
                term = lax.dot_general(
                    source, weights[j, k], (((1,), (0 if number else 1,)), ((), ())),
                    preferred_element_type=jnp.float32,
                )
                total = term if total is None else total + term
            for r in range(block_rows):
                row = j * block_rows + r
                value = total[:, r * cells:(r + 1) * cells].astype(jnp.bfloat16)
                own_v[row] = value
                if has_next:
                    if number:
                        ahead_row = ahead[0][row] if row < halo else ahead[1][row - (rows - halo)]
                    else:
                        ahead_row = ahead[0][row, mine]
                    entry_next = value.astype(jnp.float32) + ahead_row.astype(jnp.float32)
                    if row < halo:
                        up_s[row] = entry_next.astype(jnp.bfloat16)
                    if row >= rows - halo:
                        down_s[row - (rows - halo)] = entry_next.astype(jnp.bfloat16)
                elif (row + 1) % part == 0:
                    store(row // part)

    if number:
        @pl.when(flags[0] == number)
        def _():
            by_name = dict(zip(order, arrived))
            active(by_name[-2], by_name[-1], by_name[0])
    else:
        for odd in range(2):
            @pl.when((flags[0] == number) & (lax.rem(flags[1], 2) == odd))
            def _(odd=odd):
                active(arrived[1 - odd], arrived[odd])

    if not has_next:
        @pl.when(flags[0] != number)
        def _():
            for i, kept in enumerate(saved):
                @pl.when(flags[0] == i)
                def _(kept=kept):
                    copy = pltpu.make_async_copy(kept, own_v, sems.at[len(stores)])
                    copy.start()
                    copy.wait()

            for i in range(len(stores)):
                store(i)

        wait_all(stores)


def section(number, bounds, halo, flags, offsets, kappa, forcing, arrived, following, weights, saved, result):
    rows, total, cells = forcing.shape
    fields = bounds[1] - bounds[0]
    count, per_row, block, _ = weights.shape
    has_next = bool(following)
    order = ORDERS[min(number, 1)][bounds[0] > 0]
    arrived = [arrived[i] for i in order]
    operands = [flags, offsets, kappa, in_vmem(forcing)] + arrived
    operands += following
    specs = [SMEM] * 2 + [VMEM] * (len(operands) - 2)
    operands.append(in_vmem(weights))
    specs.append(VMEM)
    extent = rows + 2 * halo
    packed = packed_rows(halo, *bounds)
    scratch = [
        pltpu.VMEM((extent, fields, cells), jnp.float32),
        pltpu.VMEM(((extent - 2 * EDGE) * cells // block, fields, block), jnp.bfloat16),
    ]
    aliases = {}
    if has_next:
        outs = [jax.ShapeDtypeStruct((n, fields, cells), jnp.bfloat16) for n in (rows, halo + packed, halo + packed)]
        out_specs = [VMEM] * 3
        if packed:
            scratch.append(pltpu.VMEM((packed * fields, cells), jnp.float32))
    else:
        outs = [jax.ShapeDtypeStruct((total, rows, cells), jnp.bfloat16)]
        out_specs = [HBM]
        scratch += [
            pltpu.VMEM((rows, fields, cells), jnp.bfloat16),
            pltpu.VMEM((fields, rows, cells), jnp.bfloat16),
            pltpu.SemaphoreType.DMA((3,)),
        ]
        operands += [in_hbm(value) for value in saved]
        specs += [HBM] * len(saved)
        if result is not None:
            aliases = {len(operands): 0}
            operands.append(result)
            specs.append(HBM)
    if packed:
        outs.append(jax.ShapeDtypeStruct((extent, cells), jnp.float32))
        out_specs.append(VMEM)
    return pl.pallas_call(
        functools.partial(section_kernel, order, number, bounds, halo, len(saved), has_next),
        in_specs=specs,
        out_shape=outs,
        out_specs=out_specs,
        input_output_aliases=aliases,
        scratch_shapes=scratch,
        compiler_params=pltpu.CompilerParams(vmem_limit_bytes=LIMIT),
        cost_estimate=pl.CostEstimate(
            flops=WEIGHT * 2 * count * per_row * block * block * fields, bytes_accessed=weights.size * 2, transcendentals=0
        ),
    )(*operands)


def local(forcing, kappa, col_blocks, remap_weights):
    n_tile = lax.axis_size("tile")
    n_section = lax.axis_size("comp")
    tile_pos = lax.axis_index("tile")
    section_pos = lax.axis_index("comp")
    weights = remap_weights[0]
    count, block = weights.shape[0], weights.shape[-1]
    rows, cells = forcing.shape[-2:]
    half = count // 2
    halo = half * block // cells + EDGE
    flags = jnp.stack([section_pos, tile_pos, jnp.full_like(tile_pos, n_tile)]).astype(jnp.int32)

    def place(s, t):
        return s * n_tile + t % n_tile

    def send(value, source, target, shift):
        pairs = [(place(source, t), place(target, t + shift)) for t in range(n_tile)]
        others = [s for s in range(n_section) if s not in (source, target)]
        if n_section % 2 == 0 and source % 2:
            rest = [(target, target ^ 1), (target ^ 1, source ^ 1), (source ^ 1, source)]
            rest += [(s, s ^ 1) for s in others if s not in (target ^ 1, source ^ 1)]
        elif source ^ 1 == target and n_section % 2 == 0:
            rest = [(target, source)] + [(s, s ^ 1) for s in others]
        else:
            rest = []
        pairs += [(place(s, t), place(to, t)) for s, to in rest for t in range(n_tile)]
        return lax.ppermute(value, AXES, pairs)

    def exchange(value, first):
        pairs = [(place(0, t), place(0, t + 1 if t % 2 == first else t - 1)) for t in range(n_tile)]
        pairs += [(place(s, t), place((s - 2) % (n_section - 1) + 1, t)) for s in range(1, n_section) for t in range(n_tile)]
        return lax.ppermute(value, AXES, pairs)

    fields = forcing.reshape(-1, rows, cells)
    marks = [fields.shape[0] * sum(SHARES[:c]) // sum(SHARES) for c in range(len(SHARES) + 1)]
    by_row, narrow, *edges = prepare(flags, fields, kappa[0], halo, marks)
    weights, offsets, *edges[2:] = load(flags, col_blocks[0].T, weights, edges[2:])
    arrivals = []
    for c in range(len(SHARES)):
        arrivals.append([exchange(edges[2 * c + 1], 0), exchange(edges[2 * c], 1)])
    narrow = lax.ppermute(narrow, "comp", [(s, s ^ 1) for s in range(n_section) if s ^ 1 < n_section])
    following = [[[narrow]] * len(SHARES)] + [[pair[::-1] for pair in arrivals]] * (n_section - 2) + [[[]] * len(SHARES)]
    owns = [[] for _ in SHARES]
    result = None
    for s in range(n_section):
        last = s + 1 == n_section
        leaving = []
        rates = kappa[0]
        for c, bounds in enumerate(zip(marks[:-1], marks[1:])):
            parts = list(section(
                s, bounds, halo, flags, offsets, rates, by_row, arrivals[c], following[s][c],
                weights, owns[c] if last else [], result,
            ))
            if c == 0:
                rates = parts.pop()
            if last:
                result = parts[0]
                continue
            own, up, down = parts
            owns[c].append(own)
            leaving.append([send(part, s, s + 1, shift) for part, shift in ((own, 0), (down, 1), (up, -1))])
        arrivals = leaving
    return result.reshape(forcing.shape)


def solution(mesh):
    placed = (
        P("comp", None, None, "tile", None),
        P("comp", "tile", None),
        P("comp", "tile", None),
        P("comp", "tile", None, None, None),
    )
    return jax.shard_map(
        local,
        mesh=mesh,
        in_specs=placed,
        out_specs=P("comp", None, None, "tile", None),
        check_vma=False,
    )
```

```python
import functools

import jax
import jax.numpy as jnp
from jax import lax
from jax.experimental import pallas as pl
from jax.experimental.pallas import tpu as pltpu
from jax.sharding import PartitionSpec as P

AXES = ("comp", "tile")
SHARES = (1, 1)
PAIRS = 8
EDGE = 2
LIMIT = 24 << 20
ORDERS = (((0, 1), (0, 1)), ((-2, -1, 0), (-1, -2, 0)))
WEIGHT = 20
HBM = pl.BlockSpec(memory_space=pltpu.HBM)
VMEM = pl.BlockSpec(memory_space=pltpu.VMEM)
SMEM = pl.BlockSpec(memory_space=pltpu.SMEM)
ANY = pl.BlockSpec(memory_space=pl.ANY)


def start_all(copies):
    for copy in copies:
        copy.start()


def wait_all(copies):
    for copy in copies:
        copy.wait()


def in_hbm(value):
    return pltpu.with_memory_space_constraint(value, pltpu.HBM)


def in_vmem(value):
    return pltpu.with_memory_space_constraint(value, pltpu.VMEM)


def split(value):
    parts = []
    for _ in range(3):
        head = value.astype(jnp.bfloat16).astype(jnp.float32)
        parts.append(head)
        value = value - head
    return parts


def packed_rows(halo, start, stop):
    return 0 if start else -(-3 * halo // (stop - start))


def joined(parts, room):
    at = 0
    for part in parts:
        room[at:at + part.shape[0], :] = part
        at += part.shape[0]
    room[at:, :] = jnp.zeros((room.shape[0] - at, room.shape[1]), jnp.float32)
    return room[...].astype(jnp.bfloat16)


def prepare_kernel(halo, marks, _, forcing, kappa, *refs):
    by_row, narrow, *edges, f_v, k_v, pack, sems, k_sem = refs
    total, rows, cells = f_v.shape
    step = rows // sems.shape[0]
    loads = []
    for i in range(sems.shape[0]):
        part = pl.ds(i * step, step)
        loads.append(pltpu.make_async_copy(forcing.at[:, part], f_v.at[:, part], sems.at[i]))
    fetch = pltpu.make_async_copy(kappa, k_v, k_sem)
    fetch.start()
    start_all(loads)
    fetch.wait()
    odd = lax.rem(lax.axis_index("tile"), 2) == 1
    swapped = odd & (lax.axis_index("comp") == 0)

    def write(edges):
        parts = split(k_v[...])
        narrow[rows] = joined(parts, pack)
        for e, start in enumerate((0, rows - halo)):
            row = joined([part[start:start + halo] for part in parts], pack)
            tail = (edges[e].shape[0] - halo, *edges[e].shape[1:])
            edges[e][halo:] = row[:tail[0] * tail[1]].reshape(tail)
        for i, load in enumerate(loads):
            load.wait()
            turned = jnp.swapaxes(f_v[:, i * step:(i + 1) * step, :], 0, 1)
            by_row[i * step:(i + 1) * step] = turned
            for r in range(step):
                y = i * step + r
                value = turned[r].astype(jnp.bfloat16)
                narrow[y] = value
                for edge_first, edge_last, start, stop in zip(edges[0::2], edges[1::2], marks[:-1], marks[1:]):
                    if y < halo:
                        edge_first[y] = value[start:stop]
                    if y >= rows - halo:
                        edge_last[y - (rows - halo)] = value[start:stop]

    @pl.when(swapped)
    def _():
        write([edge for pair in zip(edges[1::2], edges[0::2]) for edge in pair])

    @pl.when(jnp.logical_not(swapped))
    def _():
        write(edges)


def prepare(flags, fields, kappa, halo, marks):
    edges = [
        jax.ShapeDtypeStruct((halo + packed_rows(halo, 0, stop - start), stop - start, kappa.shape[1]), jnp.bfloat16)
        for start, stop in zip(marks[:-1], marks[1:]) for _ in range(2)
    ]
    total, rows, cells = fields.shape
    return pl.pallas_call(
        functools.partial(prepare_kernel, halo, marks),
        in_specs=[ANY, HBM, HBM],
        out_shape=[
            pltpu.VMEM((rows, total, cells), jnp.float32),
            jax.ShapeDtypeStruct((rows + 1, total, cells), jnp.bfloat16),
        ] + edges,
        out_specs=[VMEM] * (2 + len(edges)),
        scratch_shapes=[
            pltpu.VMEM((total, rows, cells), jnp.float32),
            pltpu.VMEM(kappa.shape, kappa.dtype),
            pltpu.VMEM((total, cells), jnp.float32),
            pltpu.SemaphoreType.DMA((rows // 8,)),
            pltpu.SemaphoreType.DMA,
        ],
        compiler_params=pltpu.CompilerParams(vmem_limit_bytes=LIMIT),
        cost_estimate=pl.CostEstimate(flops=0, bytes_accessed=fields.size * 12, transcendentals=0),
    )(flags, in_hbm(fields), in_hbm(kappa))


def load_kernel(n_passed, flags, columns, weights, *refs):
    held, offsets = refs[n_passed:n_passed + 2]
    c_v, sems, c_sem = refs[-3:]
    count, per_row = weights.shape[:2]
    take = pltpu.make_async_copy(columns, c_v, c_sem)
    take.start()
    loads = [pltpu.make_async_copy(weights.at[j], held.at[j], sems.at[j]) for j in range(count)]
    start_all(loads)
    take.wait()
    ahead = c_v[...] - (flags[1] * count + lax.broadcasted_iota(jnp.int32, c_v.shape, 1)) + count // 2
    every = flags[2] * count
    ahead = jnp.where(ahead < 0, ahead + every, jnp.where(ahead >= every, ahead - every, ahead))
    offsets[...] = ahead - count // 2
    wait_all(loads)

    @pl.when(flags[0] != 0)
    def _():
        def turn(i, _):
            j, k = i // per_row, i % per_row
            held[j, k] = held[j, k].T
            return 0

        lax.fori_loop(0, count * per_row, turn, 0, unroll=4)


def load(flags, columns, weights, passed):
    return pl.pallas_call(
        functools.partial(load_kernel, len(passed)),
        in_specs=[SMEM, HBM, HBM] + [ANY] * len(passed),
        out_shape=[
            pltpu.VMEM(weights.shape, weights.dtype), jax.ShapeDtypeStruct(columns.shape, columns.dtype)
        ] + [jax.ShapeDtypeStruct(p.shape, p.dtype) for p in passed],
        out_specs=[VMEM, VMEM] + [ANY] * len(passed),
        input_output_aliases={3 + i: 2 + i for i in range(len(passed))},
        scratch_shapes=[
            pltpu.VMEM(columns.shape, columns.dtype),
            pltpu.SemaphoreType.DMA((weights.shape[0],)),
            pltpu.SemaphoreType.DMA,
        ],
        compiler_params=pltpu.CompilerParams(vmem_limit_bytes=LIMIT),
        cost_estimate=pl.CostEstimate(flops=0, bytes_accessed=weights.size * 4, transcendentals=0),
    )(flags, in_hbm(columns), in_hbm(weights), *passed)


def beside_matrix(cells):
    source = lax.broadcasted_iota(jnp.int32, (2 * cells, 2 * cells), 0)
    target = lax.broadcasted_iota(jnp.int32, (2 * cells, 2 * cells), 1)
    apart = (source - target + 2 * cells) % cells
    same = (source < cells) == (target < cells)
    return jnp.where(same & ((apart == 1) | (apart == cells - 1)), 1.0, 0.0).astype(jnp.bfloat16)


def section_kernel(order, number, bounds, halo, n_saved, has_next, flags, offsets, kappa, forcing, *refs):
    refs = list(refs)
    arrived = [refs.pop(0) for _ in order]
    start_chunk = bounds[0] == 0
    ahead = [refs.pop(0) for _ in range(2 if number else 1)] if has_next else []
    weights = refs.pop(0)
    saved = [refs.pop(0) for _ in range(n_saved)]
    if has_next:
        own_out, up_out, down_out = refs.pop(0), refs.pop(0), refs.pop(0)
    else:
        if bounds[0]:
            refs.pop(0)
        result = refs.pop(0)
    if has_next:
        own_v, up_s, down_s = own_out, up_out, down_out
    k_v = refs.pop(0) if start_chunk else kappa
    once, smooth, *rest = refs
    if not has_next:
        own_v, turned, sems = rest
    rows, _, cells = forcing.shape
    fields = bounds[1] - bounds[0]
    count, per_row = weights.shape[:2]
    block = weights.shape[-1]
    extent = rows + 2 * halo
    lo, hi = halo, halo + rows

    if not has_next:
        part = rows // 2
        stores = [
            pltpu.make_async_copy(
                turned.at[:, pl.ds(i * part, part)], result.at[pl.ds(bounds[0], fields), pl.ds(i * part, part)], sems.at[i]
            )
            for i in range(2)
        ]

        def store(i):
            turned[:, i * part:(i + 1) * part, :] = jnp.swapaxes(own_v[i * part:(i + 1) * part], 0, 1)
            stores[i].start()

    def active(upper, lower, incoming=None):
        mine = slice(*bounds)
        beside = beside_matrix(cells)
        top = jnp.where(flags[1] == 0, 0.0, 1.0)
        bottom = jnp.where(flags[1] == flags[2] - 1, 0.0, 1.0)
        if start_chunk:
            for edge, start in ((upper, 0), (lower, hi)):
                parts = edge[halo:].astype(jnp.float32).reshape(-1, cells)
                k_v[start:start + halo, :] = parts[:halo] + parts[halo:2 * halo] + parts[2 * halo:3 * halo]
            k_v[lo:hi, :] = kappa[...]

        def entry(i):
            if i < lo:
                return upper[i].astype(jnp.float32)
            if i >= hi:
                return lower[i - hi].astype(jnp.float32)
            value = forcing[i - lo, mine]
            if number:
                value = value + incoming[i - lo].astype(jnp.float32)
            return value

        def step(i, here, north, south, east_west):
            if i == lo:
                north = north * top
            if i == lo - 1:
                south = south * top
            if i == hi:
                north = north * bottom
            if i == hi - 1:
                south = south * bottom
            rate = k_v[i:i + 1, :]
            return (1.0 - 4.0 * rate) * here + rate * ((north + south) + east_west)

        def sums_beside(values):
            pairs = [
                jnp.concatenate([a.astype(jnp.bfloat16), b.astype(jnp.bfloat16)], axis=1)
                for a, b in zip(values[0::2], values[1::2])
            ]
            total = jnp.dot(jnp.concatenate(pairs, axis=0), beside, preferred_element_type=jnp.float32)
            sums = []
            for p in range(len(pairs)):
                both = total[p * fields:(p + 1) * fields]
                sums += [both[:, :cells], both[:, cells:]]
            return sums

        def sweep(fetch, start, stop, put):
            for i in range(start, stop, 2 * PAIRS):
                group = range(i, min(i + 2 * PAIRS, stop))
                values = [fetch(r) for r in group]
                sums = sums_beside(values)
                around = [fetch(i - 1)] + values + [fetch(group[-1] + 1)]
                for g, r in enumerate(group):
                    put(r, around[g], around[g + 1], around[g + 2], sums[g])

        def put_once(r, north, here, south, east_west):
            if 0 < r < extent - 1:
                once[r] = step(r, here, north, south, east_west)

        def put_smooth(r, north, here, south, east_west):
            side = slice(0, cells) if r % 2 == 0 else slice(cells, 2 * cells)
            smooth[r // 2 - 1, :, side] = step(r, here, north, south, east_west).astype(jnp.bfloat16)

        sweep(lambda r: entry(r) if 0 <= r < extent else None, 0, extent, put_once)
        sweep(lambda r: once[r], 2, extent - 2, put_smooth)

        half = (halo - EDGE) * cells // block
        block_rows = block // cells
        if has_next and start_chunk:
            pack, = rest
            if number:
                up_s[halo:] = ahead[0][halo:]
                down_s[halo:] = ahead[1][halo:]
            else:
                parts = ahead[0][rows].astype(jnp.float32)
                parts = [parts[p * rows:(p + 1) * rows] for p in range(3)]
                tail = (up_s.shape[0] - halo, fields, cells)
                up_s[halo:] = joined([part[:halo] for part in parts], pack).reshape(tail)
                down_s[halo:] = joined([part[rows - halo:] for part in parts], pack).reshape(tail)
        for j in range(count):
            sources = [smooth[offsets[k, j] + (j + half)] for k in range(per_row)]
            if number:
                total = jnp.dot(
                    jnp.concatenate(sources, axis=1), weights[j].reshape(per_row * block, block),
                    preferred_element_type=jnp.float32,
                )
            else:
                total = None
                for k in range(per_row):
                    term = lax.dot_general(
                        sources[k], weights[j, k], (((1,), (1,)), ((), ())), preferred_element_type=jnp.float32
                    )
                    total = term if total is None else total + term
            for r in range(block_rows):
                row = j * block_rows + r
                value = total[:, r * cells:(r + 1) * cells].astype(jnp.bfloat16)
                own_v[row] = value
                if has_next:
                    if number:
                        ahead_row = ahead[0][row] if row < halo else ahead[1][row - (rows - halo)]
                    else:
                        ahead_row = ahead[0][row, mine]
                    entry_next = value.astype(jnp.float32) + ahead_row.astype(jnp.float32)
                    if row < halo:
                        up_s[row] = entry_next.astype(jnp.bfloat16)
                    if row >= rows - halo:
                        down_s[row - (rows - halo)] = entry_next.astype(jnp.bfloat16)
                elif (row + 1) % part == 0:
                    store(row // part)

    if number:
        @pl.when(flags[0] == number)
        def _():
            by_name = dict(zip(order, arrived))
            active(by_name[-2], by_name[-1], by_name[0])
    else:
        for odd in range(2):
            @pl.when((flags[0] == number) & (lax.rem(flags[1], 2) == odd))
            def _(odd=odd):
                active(arrived[1 - odd], arrived[odd])

    if not has_next:
        @pl.when(flags[0] != number)
        def _():
            for i, kept in enumerate(saved):
                @pl.when(flags[0] == i)
                def _(kept=kept):
                    copy = pltpu.make_async_copy(kept, own_v, sems.at[len(stores)])
                    copy.start()
                    copy.wait()

            for i in range(len(stores)):
                store(i)

        wait_all(stores)


def section(number, bounds, halo, flags, offsets, kappa, forcing, arrived, following, weights, saved, result):
    rows, total, cells = forcing.shape
    fields = bounds[1] - bounds[0]
    count, per_row, block, _ = weights.shape
    has_next = bool(following)
    order = ORDERS[min(number, 1)][bounds[0] > 0]
    arrived = [arrived[i] for i in order]
    operands = [flags, offsets, kappa, in_vmem(forcing)] + arrived
    operands += following
    specs = [SMEM] * 2 + [VMEM] * (len(operands) - 2)
    operands.append(in_vmem(weights))
    specs.append(VMEM)
    extent = rows + 2 * halo
    packed = packed_rows(halo, *bounds)
    scratch = [
        pltpu.VMEM((extent, fields, cells), jnp.float32),
        pltpu.VMEM(((extent - 2 * EDGE) * cells // block, fields, block), jnp.bfloat16),
    ]
    aliases = {}
    if has_next:
        outs = [jax.ShapeDtypeStruct((n, fields, cells), jnp.bfloat16) for n in (rows, halo + packed, halo + packed)]
        out_specs = [VMEM] * 3
        if packed:
            scratch.append(pltpu.VMEM((packed * fields, cells), jnp.float32))
    else:
        outs = [jax.ShapeDtypeStruct((total, rows, cells), jnp.bfloat16)]
        out_specs = [HBM]
        scratch += [
            pltpu.VMEM((rows, fields, cells), jnp.bfloat16),
            pltpu.VMEM((fields, rows, cells), jnp.bfloat16),
            pltpu.SemaphoreType.DMA((3,)),
        ]
        operands += [in_hbm(value) for value in saved]
        specs += [HBM] * len(saved)
        if result is not None:
            aliases = {len(operands): 0}
            operands.append(result)
            specs.append(HBM)
    if packed:
        outs.append(jax.ShapeDtypeStruct((extent, cells), jnp.float32))
        out_specs.append(VMEM)
    return pl.pallas_call(
        functools.partial(section_kernel, order, number, bounds, halo, len(saved), has_next),
        in_specs=specs,
        out_shape=outs,
        out_specs=out_specs,
        input_output_aliases=aliases,
        scratch_shapes=scratch,
        compiler_params=pltpu.CompilerParams(vmem_limit_bytes=LIMIT),
        cost_estimate=pl.CostEstimate(
            flops=WEIGHT * 2 * count * per_row * block * block * fields, bytes_accessed=weights.size * 2, transcendentals=0
        ),
    )(*operands)


def local(forcing, kappa, col_blocks, remap_weights):
    n_tile = lax.axis_size("tile")
    n_section = lax.axis_size("comp")
    tile_pos = lax.axis_index("tile")
    section_pos = lax.axis_index("comp")
    weights = remap_weights[0]
    count, block = weights.shape[0], weights.shape[-1]
    rows, cells = forcing.shape[-2:]
    half = count // 2
    halo = half * block // cells + EDGE
    flags = jnp.stack([section_pos, tile_pos, jnp.full_like(tile_pos, n_tile)]).astype(jnp.int32)

    def place(s, t):
        return s * n_tile + t % n_tile

    def send(value, source, target, shift):
        pairs = [(place(source, t), place(target, t + shift)) for t in range(n_tile)]
        others = [s for s in range(n_section) if s not in (source, target)]
        if n_section % 2 == 0 and source % 2:
            rest = [(target, target ^ 1), (target ^ 1, source ^ 1), (source ^ 1, source)]
            rest += [(s, s ^ 1) for s in others if s not in (target ^ 1, source ^ 1)]
        elif source ^ 1 == target and n_section % 2 == 0:
            rest = [(target, source)] + [(s, s ^ 1) for s in others]
        else:
            rest = []
        pairs += [(place(s, t), place(to, t)) for s, to in rest for t in range(n_tile)]
        return lax.ppermute(value, AXES, pairs)

    def exchange(value, first):
        pairs = [(place(0, t), place(0, t + 1 if t % 2 == first else t - 1)) for t in range(n_tile)]
        pairs += [(place(s, t), place((s - 2) % (n_section - 1) + 1, t)) for s in range(1, n_section) for t in range(n_tile)]
        return lax.ppermute(value, AXES, pairs)

    fields = forcing.reshape(-1, rows, cells)
    marks = [fields.shape[0] * sum(SHARES[:c]) // sum(SHARES) for c in range(len(SHARES) + 1)]
    by_row, narrow, *edges = prepare(flags, fields, kappa[0], halo, marks)
    weights, offsets, *edges[2:] = load(flags, col_blocks[0].T, weights, edges[2:])
    arrivals = []
    for c in range(len(SHARES)):
        arrivals.append([exchange(edges[2 * c + 1], 0), exchange(edges[2 * c], 1)])
    narrow = lax.ppermute(narrow, "comp", [(s, s ^ 1) for s in range(n_section) if s ^ 1 < n_section])
    following = [[[narrow]] * len(SHARES)] + [[pair[::-1] for pair in arrivals]] * (n_section - 2) + [[[]] * len(SHARES)]
    owns = [[] for _ in SHARES]
    result = None
    for s in range(n_section):
        last = s + 1 == n_section
        leaving = []
        rates = kappa[0]
        for c, bounds in enumerate(zip(marks[:-1], marks[1:])):
            parts = list(section(
                s, bounds, halo, flags, offsets, rates, by_row, arrivals[c], following[s][c],
                weights, owns[c] if last else [], result,
            ))
            if c == 0:
                rates = parts.pop()
            if last:
                result = parts[0]
                continue
            own, up, down = parts
            owns[c].append(own)
            leaving.append([send(part, s, s + 1, shift) for part, shift in ((own, 0), (down, 1), (up, -1))])
        arrivals = leaving
    return result.reshape(forcing.shape)


def solution(mesh):
    placed = (
        P("comp", None, None, "tile", None),
        P("comp", "tile", None),
        P("comp", "tile", None),
        P("comp", "tile", None, None, None),
    )
    return jax.shard_map(
        local,
        mesh=mesh,
        in_specs=placed,
        out_specs=P("comp", None, None, "tile", None),
        check_vma=False,
    )
```
